1024 devices in a mesh: dp: 4 (over z_hi), expert: 32 (over x, y), tensor: 8 (over z_lo, core).
Axes of the slice: x: 4, y: 8, z: 16 (z_hi: 4, z_lo: 4; z = z_hi * 4 + z_lo), core: 2. Of those that a mesh axis runs over, the one named last changes fastest.
Arguments:
- context: bfloat16 [32768, 4096], P(('dp', 'expert'), 'tensor'), parts along dimension 0, may hold values from -6 to 6
- out_weight: bfloat16 [4096, 7168], P('tensor'), may hold values from -0.09375 to 0.09375
- attn_bias: bfloat16 [7168], replicated, may hold values from -3 to 3
- residual: bfloat16 [32768, 7168], P(('dp', 'expert', 'tensor')), parts along dimension 0, may hold values from -6 to 6
- dropout_bits: int32 [32768, 448], P(('dp', 'expert', 'tensor')), parts along dimension 0, may hold values from 0 to 65535, as said below
- norm_gain: bfloat16 [7168], replicated, may hold values from 0.5 to 1.5
- routes: int32 [32768, 2], P(('dp', 'expert', 'tensor')), parts along dimension 0, may hold values from 0 to 63, all different within a row; in each aligned block of 32 rows (0 to 31, 32 to 63, ...) at most 2 rows name the same one
Outputs:
- hidden_state: bfloat16 [32768, 7168], P(('dp', 'expert', 'tensor')), parts along dimension 0
- dispatched: bfloat16 [128, 8, 64, 2, 7168], P('dp', 'tensor', 'expert'), parts along dimension 0
The draws below stay inside these ranges and needn't reach their ends.
There are 4 independent parts, one for each index of `dp`. The reference program is written for one: setup_inputs(seed, part) draws one part's arguments, and reference() takes and returns one part's arrays. A program takes and returns all parts, laid end to end along the dimension named above; an argument that names none is the same for every part. Nothing has to cross between parts.
Inputs may be any that keep to these rules, and one draw needn't show every extreme that they name: `routes`: each row names two different experts; within the 32 rows of one device no expert is named more than 2 times. `dropout_bits`: bit b of word w of a row is 1 where feature 16 w + b is kept; each word uses its 16 lowest bits.
All inputs are finite; a program needn't handle non-finite values.
Results may differ from the reference program's by a relative error of at most 0.015.
Values may be sent and summed in bfloat16 or wider, within the bound.
A program may use at most 64 MiB of HBM per device.

```python
import math
import jax
import jax.numpy as jnp
import numpy as np
from jax import lax

D = 7168
HEAD = 128
TOK_DEV = 32
HEADS = 32
EXPERTS = 64
CAP = 2
TOKENS = 8192
N_EXPERT = 32
N_TENSOR = 8


def draw_dropout_bits(key, part):
    key = jax.random.fold_in(key, 7)
    digits = jax.random.randint(key, (TOKENS, D // 16, 16), 0, 10)
    kept = (digits != 0).astype(jnp.int32)
    powers = jnp.left_shift(jnp.ones((16,), jnp.int32), jnp.arange(16, dtype=jnp.int32))
    return jnp.sum(kept * powers, axis=-1).astype(jnp.int32)


def spiked(values, rng, source, target, blocks, factor):
    owner, partner = [(jnp.arange(values.shape[dim]) // (values.shape[dim] // blocks)).reshape([-1 if axis == dim else 1 for axis in range(values.ndim)]) for dim in (source, target)]
    chosen = jax.random.permutation(rng, blocks)[partner]
    strong = (owner == chosen) | (owner == (partner + blocks // 2) % blocks)
    return jnp.where(strong, factor * values, values)


def block_scale(stream_key, extent, cuts, smallest, top_value):
    loudness, own = 1.0, jax.random.fold_in(stream_key, 6)
    for axis_at, shards_of in cuts:
        steps = jnp.exp(jax.random.uniform(jax.random.fold_in(own, axis_at), (shards_of,), jnp.float32, smallest / len(cuts), top_value / len(cuts)))
        loudness = loudness * jnp.repeat(steps, extent[axis_at] // shards_of).reshape([-1 if axis == axis_at else 1 for axis in range(len(extent))])
    return loudness


def deal_out(own_key, own, number, rows, count, top, bound, lean):
    ranking = jax.random.permutation(own_key, count)
    crowded, common = load_shares(count, rows * top, bound, lean, True), load_shares(count, rows * top, bound, lean, False)
    places = jnp.arange(count)

    def named(lengths, rotation):
        used = int((lengths > 0).sum())
        fixed = max(1, used // 4)
        shifted = fixed + (places - fixed + rotation * (used - fixed)) % max(1, count - fixed)
        return jnp.zeros((count,), jnp.int32).at[ranking[jnp.where(places < fixed, places, shifted)]].set(jnp.asarray(lengths, jnp.int32))

    lengths = jnp.where(number % 4 == 0, named(crowded, number // 4), named(common, number - number // 4 - 1))
    mixed = jax.random.permutation(jax.random.fold_in(own, 3), count)
    giver, taker = mixed[0:count // 2 * 2:2], mixed[1:count // 2 * 2:2]
    room = jnp.minimum(lengths[giver] - 1, bound - lengths[taker]) // 2
    room = jnp.where((giver == ranking[0]) | (taker == ranking[0]) | (lengths[taker] == 0), 0, jnp.maximum(room, 0))
    shifted = jax.random.randint(jax.random.fold_in(own, 4), (count // 2,), 0, 1 << 20) % (room + 1)
    lengths = lengths.at[giver].add(-shifted).at[taker].add(shifted)
    labels = jnp.searchsorted(jnp.cumsum(lengths), jnp.arange(rows * top), side="right").astype(jnp.int32)
    listing = labels.reshape(top, rows).T
    listing = listing[jax.random.permutation(jax.random.fold_in(own, 1), rows)]
    rotation = jax.random.randint(jax.random.fold_in(own, 2), (rows, 1), 0, top)
    return jnp.take_along_axis(listing, (jnp.arange(top)[None, :] + rotation) % top, axis=1)


def load_shares(count, total, most, slope, full):
    portions = [(1 << 20) // math.isqrt(grade ** slope) + 1 for grade in range(1, count + 1)]
    largest = most if full else min(most, max(-(-total // count), total * portions[0] // sum(portions)))
    least = 1 if total - largest >= count - 1 else 0
    counts, rest = [largest] + [least] * (count - 1), total - largest - least * (count - 1)
    while rest > 0:
        free = [i for i in range(1, count) if counts[i] < largest] or [i for i in range(1, count) if counts[i] < most]
        pool, budget = sum([portions[i] for i in free]), rest
        for i in free:
            extra = min(most - counts[i], max(1, budget * portions[i] // pool), rest)
            counts[i] = counts[i] + extra
            rest = rest - extra
    return np.array(counts)


def bell_draw(own_key, shape, deviation, most, pieces=(), held_as=jnp.bfloat16):
    drawn = jax.random.normal(own_key, shape, jnp.float32) * deviation
    if len(pieces) > 0:
        drawn = block_scale(own_key, shape, pieces, -0.22, 0.18) * drawn
    return jnp.clip(drawn, min=-most, max=most).astype(held_as)


def noise_with(stream_key, extent, deviation, limit, shards, heavy, kind=jnp.bfloat16):
    result = deviation * jax.random.normal(stream_key, extent, jnp.float32)
    if shards:
        result = result * block_scale(stream_key, extent, shards, -0.22, 0.18)
    return jnp.clip(spiked(result, jax.random.fold_in(stream_key, 3), *heavy), -limit, limit).astype(kind)


def setup_inputs(seed: int = 0, part: int = 0) -> dict:
    key_of = jax.random.split(jax.random.key(seed), 8)
    part_keys = jax.random.split(jax.random.fold_in(key_of[7], part), 8)
    context = noise_with(part_keys[0], (TOKENS, HEADS * HEAD), 1.0, 6.0, ((0, 32), (1, 8)), (1, 0, 32, 2.75))
    out_weight = bell_draw(key_of[1], (HEADS * HEAD, D), (HEADS * HEAD) ** -0.5, 0.09375, ((0, 8),))
    attn_bias = bell_draw(key_of[2], (D,), 0.5, 3.0)
    residual = bell_draw(part_keys[3], (TOKENS, D), 1.0, 6.0, ((0, 256),))
    dropout_bits = draw_dropout_bits(jax.random.fold_in(jax.random.fold_in(key_of[7], part), 71), part)
    norm_gain = jnp.clip(1.0 + 0.1 * jax.random.normal(key_of[5], (D,), jnp.float32), 0.5, 1.5).astype(jnp.bfloat16)
    routes_keys = jax.random.split(jax.random.fold_in(part_keys[6], 1), TOKENS // TOK_DEV)
    routes_turns = jax.random.permutation(jax.random.fold_in(part_keys[6], 3), TOKENS // TOK_DEV)
    routes = jax.vmap(lambda own, number: deal_out(jax.random.fold_in(part_keys[6], 2), own, number, TOK_DEV, EXPERTS, 2, CAP, 2))(routes_keys, routes_turns).reshape((TOKENS, 2))
    return {"context": context, "out_weight": out_weight, "attn_bias": attn_bias, "residual": residual, "dropout_bits": dropout_bits, "norm_gain": norm_gain, "routes": routes}


keep_scale = 1.0 / 0.9
eps_norm = 1e-05

def reference(context, out_weight, attn_bias, residual, dropout_bits, norm_gain, routes):
    head_width = out_weight.shape[0] // N_TENSOR
    total = jnp.zeros((context.shape[0], out_weight.shape[1]), jnp.float32)
    for group in range(N_TENSOR):
        lower = group * head_width
        product = jnp.dot(context[:, lower:lower + head_width], out_weight[lower:lower + head_width], preferred_element_type=jnp.float32)
        total = total + lax.optimization_barrier(product.astype(jnp.bfloat16)).astype(jnp.float32)
    attention = total.astype(jnp.bfloat16)
    word_rows = jnp.repeat(dropout_bits, 16, axis=1)
    offsets = lax.broadcasted_iota(jnp.int32, word_rows.shape, 1) % 16
    keep_mask = jnp.bitwise_and(jnp.right_shift(word_rows, offsets), 1).astype(jnp.float32)
    hidden_state = (residual.astype(jnp.float32) + keep_mask * (attention.astype(jnp.float32) + attn_bias.astype(jnp.float32)) * keep_scale).astype(jnp.bfloat16)
    hidden_float = hidden_state.astype(jnp.float32)
    mean_square = lax.optimization_barrier(jnp.mean(hidden_float * hidden_float, axis=-1, keepdims=True))
    normed = (hidden_float * lax.rsqrt(mean_square + eps_norm) * norm_gain.astype(jnp.float32)).astype(jnp.bfloat16)
    device_count = TOKENS // TOK_DEV
    routes_dev = routes.reshape(device_count, TOK_DEV * 2)
    onehot = (routes_dev[:, :, None] == jnp.arange(EXPERTS, dtype=jnp.int32)[None, None, :]).astype(jnp.int32)
    earlier = jnp.cumsum(onehot, axis=1) - onehot
    slot_index = lax.optimization_barrier(jnp.sum(earlier * onehot, axis=2)).astype(jnp.int32)
    positions = (routes_dev * CAP + slot_index).reshape(device_count, TOK_DEV, 2)
    normed_dev = normed.reshape(device_count, TOK_DEV, D)
    buffer = jnp.zeros((device_count, EXPERTS * CAP, D), jnp.bfloat16)
    device_ids = jnp.arange(device_count, dtype=jnp.int32)[:, None]
    for which in range(2):
        buffer = buffer.at[device_ids, positions[:, :, which]].set(normed_dev)
    dispatched = buffer.reshape(N_EXPERT, N_TENSOR, EXPERTS, CAP, D)
    return (hidden_state, dispatched)
```

```python
import functools

import jax
import jax.numpy as jnp
from jax import lax
from jax.experimental import pallas as pl
from jax.experimental.pallas import tpu as pltpu
from jax.sharding import PartitionSpec as P

MESH = pl.DeviceIdType.MESH
KEEP_SCALE = 1.0 / 0.9
EPS = 1e-05
BF16 = jnp.bfloat16
F32 = jnp.float32

STRIP = 256


def iota(shape, dim):
    return lax.broadcasted_iota(jnp.int32, shape, dim)


def kernel(
    owners, groups, features,
    ctx_hbm, w_hbm, bias_ref, res_hbm, bits_hbm, routes_ref,
    hid_hbm, raw_hbm, scl_hbm,
    ctx_s, w_s, a_send, a_own, a_recv, b_send, b_recv, b_keep, c_send, c_recv, c_keep,
    res_s, bits_s, mask_s, hid_s, select_s, slots_s, squares_s, x_send, scl_s,
    ctx_sem, w_sem, res_sem, bits_sem, hid_sem, own_sem, own_scl_sem,
    a_ssem, a_rsem, b_ssem, b_rsem, c_ssem, c_rsem, x_ssem, x_rsem, s_ssem, s_rsem,
):
    quarter = features // 4
    chunks = quarter // STRIP
    expert = lax.axis_index("expert")
    tensor = lax.axis_index("tensor")
    chip = tensor // 2
    core = tensor % 2
    sibling = chip * 2 + (1 - core)
    chip1 = chip + 1 - 2 * (chip % 2)
    chip2 = (chip + 2) % 4
    chip3 = 3 - chip
    partner1 = chip1 * 2 + core
    partner2 = chip2 * 2 + core

    barrier = pltpu.get_barrier_semaphore()
    for peer in (sibling, partner1, partner2):
        pl.semaphore_signal(barrier, inc=1, device_id={"tensor": peer}, device_id_type=MESH)

    @pl.loop(1, owners)
    def _(i):
        peer = (expert + i) % owners
        pl.semaphore_signal(barrier, inc=1, device_id={"expert": peer}, device_id_type=MESH)

    ctx_copies = []
    for half, c_own in ((0, 1 - core), (1, core)):
        for place, dest in enumerate((chip3, chip1, chip2, chip)):
            rows = pl.ds(pl.multiple_of((dest * 2 + c_own) * 32, 32), 32)
            ctx_copies.append(
                pltpu.make_async_copy(
                    ctx_hbm.at[rows, :],
                    ctx_s.at[pl.ds(half * 128 + place * 32, 32), :],
                    ctx_sem.at[half * 4 + place],
                )
            )
    for copy in ctx_copies:
        copy.start()

    def w_copy(k, q):
        cols = pl.ds(pl.multiple_of(q * quarter + k * STRIP, 128), STRIP)
        return pltpu.make_async_copy(
            w_hbm.at[:, cols], w_s.at[k, :, pl.ds(q * STRIP, STRIP)], w_sem.at[k, q]
        )

    @pl.loop(0, chunks)
    def _(k):
        for q in range(4):
            w_copy(k, q).start()

    res_copy = pltpu.make_async_copy(res_hbm, res_s, res_sem)
    res_copy.start()
    bits_copy = pltpu.make_async_copy(bits_hbm, bits_s, bits_sem)
    bits_copy.start()

    def matmul(k):
        for q in range(4):
            w_copy(k, q).wait()
        part = jnp.dot(ctx_s[...], w_s[k], preferred_element_type=F32).astype(BF16)
        a_send[k] = part[:128]
        a_own[k] = part[128:]

    def remote(src, dst, ssem, rsem, peer):
        return pltpu.make_async_remote_copy(
            src_ref=src, dst_ref=dst, send_sem=ssem, recv_sem=rsem,
            device_id={"tensor": peer}, device_id_type=MESH,
        )

    def a_copy(k):
        return remote(a_send.at[k], a_recv.at[k], a_ssem.at[k], a_rsem.at[k], sibling)

    def b_copy(k):
        return remote(b_send.at[k], b_recv.at[k], b_ssem.at[k], b_rsem.at[k], partner1)

    def c_copy(k):
        return remote(c_send.at[k], c_recv.at[k], c_ssem.at[k], c_rsem.at[k], partner2)

    def stage_b(k):
        a_copy(k).wait_recv()
        b_send[k] = (a_own[k, :64].astype(F32) + a_recv[k, :64].astype(F32)).astype(BF16)
        b_copy(k).start()
        b_keep[k] = a_own[k, 64:].astype(F32) + a_recv[k, 64:].astype(F32)

    def stage_c(k):
        b_copy(k).wait_recv()
        c_send[k] = (b_keep[k, :32] + b_recv[k, :32].astype(F32)).astype(BF16)
        c_copy(k).start()
        c_keep[k] = b_keep[k, 32:] + b_recv[k, 32:].astype(F32)

    def stage_x(k):
        c_copy(k).wait_recv()
        pieces = []
        for q in range(4):
            cols = pl.ds(pl.multiple_of(q * quarter + k * STRIP, 128), STRIP)
            lanes = pl.ds(q * STRIP, STRIP)
            total = c_keep[k, :, lanes] + c_recv[k, :, lanes].astype(F32)
            attention = total.astype(BF16).astype(F32)
            hidden = (
                res_s[:, cols].astype(F32)
                + (attention + bias_ref[:, cols].astype(F32)) * mask_s[:, cols]
            ).astype(BF16)
            hid_s[:, cols] = hidden
            value = hidden.astype(F32)
            square = value * value
            folded = square[:, :128]
            for i in range(1, STRIP // 128):
                folded = folded + square[:, i * 128:(i + 1) * 128]
            squares_s[...] += folded
            pieces.append(hidden)
        stacked = jnp.concatenate(pieces, axis=0)
        picked = jnp.dot(select_s[...], stacked, preferred_element_type=F32).astype(BF16)
        cols = pl.ds(pl.multiple_of(k * STRIP, 128), STRIP)
        x_send[:, :, cols] = picked.reshape(owners, 16, STRIP)

        @pl.loop(1, owners)
        def _(i):
            peer = (expert + i) % owners
            pltpu.make_async_remote_copy(
                src_ref=x_send.at[peer, :, cols], dst_ref=raw_hbm.at[expert, :, cols],
                send_sem=x_ssem, recv_sem=x_rsem,
                device_id={"expert": peer}, device_id_type=MESH,
            ).start()

    for copy in ctx_copies:
        copy.wait()
    matmul(0)
    pl.semaphore_wait(barrier, owners + 2)
    a_copy(0).start()
    matmul(1)
    a_copy(1).start()
    stage_b(0)

    same_token = iota((32, 128), 1) % 32 == iota((32, 128), 0)
    first = jnp.sum(jnp.where(same_token, routes_ref[:, 0:1], 0), axis=0, keepdims=True)
    second = jnp.sum(jnp.where(same_token, routes_ref[:, 1:2], 0), axis=0, keepdims=True)
    j0, j1 = iota((128, 128), 0), iota((128, 128), 1)
    before = jnp.where((j0 // 32 == j1 // 32) & (j0 % 32 < j1 % 32), 1.0, 0.0).astype(BF16)

    def chosen(named, slot):
        hits = jnp.where((first == named) | (second == named), 1.0, 0.0)
        earlier = jnp.dot(hits.astype(BF16), before, preferred_element_type=F32)
        return jnp.where(earlier == slot.astype(F32), hits, 0.0)

    row, lane = iota((owners * 16, 128), 0), iota((owners * 16, 128), 1)
    picks = chosen(2 * (row // 16) + (row % 4) // 2, row % 2)
    select_s[...] = jnp.where((row // 4) % 4 == lane // 32, picks, 0.0).astype(BF16)
    row, lane = iota((owners, 128), 0), iota((owners, 128), 1)
    for slot in range(4):
        picks = chosen(2 * row + slot // 2, jnp.full((owners, 128), slot % 2, jnp.int32))
        slots_s[slot] = jnp.where(lane < 32, picks, 0.0)

    bits_copy.wait()
    squares_s[...] = jnp.zeros_like(squares_s)
    words = features // 16
    for start in range(0, words, 128):
        count = min(128, words - start)
        block = bits_s[:, start:start + count]
        low = (block % 256).astype(F32).astype(BF16)
        high = (block // 256).astype(F32).astype(BF16)
        spread_row, spread_col = iota((count, count * 16), 0), iota((count, count * 16), 1)
        here = spread_col // 16 == spread_row
        is_low = spread_col % 16 < 8
        spread_low = jnp.where(here & is_low, 1.0, 0.0).astype(BF16)
        spread_high = jnp.where(here & jnp.logical_not(is_low), 1.0, 0.0).astype(BF16)
        byte = jnp.dot(low, spread_low, preferred_element_type=F32) + jnp.dot(
            high, spread_high, preferred_element_type=F32
        )
        shift = iota(byte.shape, 1) % 8
        bit = jnp.bitwise_and(jnp.right_shift(byte.astype(jnp.int32), shift), 1)
        mask_s[:, start * 16:(start + count) * 16] = bit.astype(F32) * KEEP_SCALE
    res_copy.wait()

    @pl.loop(0, chunks + 1)
    def _(t):
        @pl.when(t >= 1)
        def _():
            stage_x(t - 1)

        @pl.when(t < chunks)
        def _():
            stage_c(t)

        @pl.when(t + 1 < chunks)
        def _():
            stage_b(t + 1)

        @pl.when(t + 2 < chunks)
        def _():
            matmul(t + 2)
            a_copy(t + 2).start()

    mean = jnp.sum(squares_s[...], axis=1, keepdims=True) / features
    scale = lax.rsqrt(mean + EPS)
    scale_row = jnp.sum(jnp.where(same_token, scale, 0.0), axis=0, keepdims=True)
    packed = jnp.zeros((owners, 128), F32)
    for slot in range(4):
        value = jnp.sum(slots_s[slot] * scale_row, axis=1, keepdims=True)
        packed = packed + jnp.where(lane == slot, value, 0.0)
    scl_s[...] = packed.reshape(owners, 1, 128)

    @pl.loop(1, owners)
    def _(i):
        peer = (expert + i) % owners
        pltpu.make_async_remote_copy(
            src_ref=scl_s.at[peer], dst_ref=scl_hbm.at[expert],
            send_sem=s_ssem, recv_sem=s_rsem,
            device_id={"expert": peer}, device_id_type=MESH,
        ).start()

    hid_copy = pltpu.make_async_copy(hid_s, hid_hbm, hid_sem)
    hid_copy.start()
    own_copy = pltpu.make_async_copy(x_send.at[expert], raw_hbm.at[expert], own_sem)
    own_copy.start()
    own_scl = pltpu.make_async_copy(scl_s.at[expert], scl_hbm.at[expert], own_scl_sem)
    own_scl.start()

    @pl.loop(0, chunks)
    def _(k):
        a_copy(k).wait_send()
        b_copy(k).wait_send()
        c_copy(k).wait_send()

    others = pl.ds(0, owners - 1)
    pltpu.make_async_copy(x_send.at[others], x_send.at[others], x_ssem).wait()
    pltpu.make_async_copy(scl_s.at[others], scl_s.at[others], s_ssem).wait()
    pltpu.make_async_copy(raw_hbm.at[others], raw_hbm.at[others], x_rsem).wait()
    pltpu.make_async_copy(scl_hbm.at[others], scl_hbm.at[others], s_rsem).wait()
    hid_copy.wait()
    own_copy.wait()
    own_scl.wait()


def local(owners, groups, context, out_weight, attn_bias, residual, dropout_bits, norm_gain, routes):
    depth, features = out_weight.shape
    rows = context.shape[0]
    tokens = residual.shape[0]
    quarter = features // 4
    chunks = quarter // STRIP
    wide = 4 * STRIP
    vmem, dma = pltpu.VMEM, pltpu.SemaphoreType.DMA
    hidden, raw, scales = pl.pallas_call(
        functools.partial(kernel, owners, groups, features),
        out_shape=(
            jax.ShapeDtypeStruct((tokens, features), BF16),
            jax.ShapeDtypeStruct((owners, 16, quarter), BF16),
            jax.ShapeDtypeStruct((owners, 1, 128), F32),
        ),
        in_specs=[
            pl.BlockSpec(memory_space=pl.ANY),
            pl.BlockSpec(memory_space=pl.ANY),
            pl.BlockSpec(memory_space=pltpu.VMEM),
            pl.BlockSpec(memory_space=pl.ANY),
            pl.BlockSpec(memory_space=pl.ANY),
            pl.BlockSpec(memory_space=pltpu.VMEM),
        ],
        out_specs=[pl.BlockSpec(memory_space=pl.ANY)] * 3,
        scratch_shapes=[
            vmem((rows, depth), BF16),
            vmem((chunks, depth, wide), BF16),
            vmem((chunks, 128, wide), BF16),
            vmem((chunks, 128, wide), BF16),
            vmem((chunks, 128, wide), BF16),
            vmem((chunks, 64, wide), BF16),
            vmem((chunks, 64, wide), BF16),
            vmem((chunks, 64, wide), F32),
            vmem((chunks, 32, wide), BF16),
            vmem((chunks, 32, wide), BF16),
            vmem((chunks, 32, wide), F32),
            vmem((tokens, features), BF16),
            vmem((tokens, features // 16), jnp.int32),
            vmem((tokens, features), F32),
            vmem((tokens, features), BF16),
            vmem((owners * 16, 128), BF16),
            vmem((4, owners, 128), F32),
            vmem((tokens, 128), F32),
            vmem((owners, 16, quarter), BF16),
            vmem((owners, 1, 128), F32),
            dma((8,)),
            dma((chunks, 4)),
            dma, dma, dma, dma, dma,
            dma((chunks,)), dma((chunks,)),
            dma((chunks,)), dma((chunks,)),
            dma((chunks,)), dma((chunks,)),
            dma, dma, dma, dma,
        ],
        compiler_params=pltpu.CompilerParams(
            collective_id=0, has_side_effects=True, vmem_limit_bytes=48 * 1024 * 1024
        ),
        cost_estimate=pl.CostEstimate(
            flops=2 * rows * depth * features,
            bytes_accessed=2 * depth * features,
            transcendentals=0,
        ),
    )(context, out_weight, attn_bias.reshape(1, -1), residual, dropout_bits, routes)
    placed = raw.reshape(owners, 4, 4, quarter).transpose(0, 2, 1, 3).reshape(owners, 4, features)
    scale = scales[:, 0, :4]
    normed = (
        placed.astype(F32) * scale[:, :, None] * norm_gain.astype(F32)[None, None, :]
    ).astype(BF16)
    return hidden, normed.reshape(owners, 1, 2, 2, features)


def solution(mesh):
    owners, groups = mesh.shape["expert"], mesh.shape["tensor"]
    tokens_split = P(("dp", "expert", "tensor"), None)
    return jax.shard_map(
        functools.partial(local, owners, groups),
        mesh=mesh,
        in_specs=(
            P(("dp", "expert"), "tensor"), P("tensor", None), P(),
            tokens_split, tokens_split, P(), tokens_split,
        ),
        out_specs=(tokens_split, P("dp", "tensor", "expert", None, None)),
        check_vma=False,
    )
```

```python
import functools

import jax
import jax.numpy as jnp
from jax import lax
from jax.experimental import pallas as pl
from jax.experimental.pallas import tpu as pltpu
from jax.sharding import PartitionSpec as P

MESH = pl.DeviceIdType.MESH
KEEP_SCALE = 1.0 / 0.9
EPS = 1e-05
BF16 = jnp.bfloat16
F32 = jnp.float32

STRIP = 256
FINAL = 256


def iota(shape, dim):
    return lax.broadcasted_iota(jnp.int32, shape, dim)


def kernel(
    owners, groups, features,
    ctx_hbm, w_hbm, bias_hbm, res_hbm, bits_hbm, routes_hbm,
    hid_s, x_recv, scl_r,
    ctx_s, w_s, a_send, a_own, a_recv, b_send, b_recv, b_keep, c_send, c_recv, c_keep,
    res_s, bits_s, mask_s, select_s, slots_s, squares_s, x_send, scl_s,
    bias_b, routes_s, bias_s,
    ctx_sem, w_sem, res_sem, bits_sem, small_sem, own_sem, own_scl_sem,
    a_ssem, a_rsem, b_ssem, b_rsem, c_ssem, c_rsem, x_ssem, x_rsem, s_ssem, s_rsem,
):
    quarter = features // 4
    chunks = quarter // STRIP
    expert = lax.axis_index("expert")
    tensor = lax.axis_index("tensor")
    chip = tensor // 2
    core = tensor % 2
    sibling = chip * 2 + (1 - core)
    chip1 = chip + 1 - 2 * (chip % 2)
    chip2 = (chip + 2) % 4
    chip3 = 3 - chip
    partner1 = chip1 * 2 + core
    partner2 = chip2 * 2 + core

    barrier = pltpu.get_barrier_semaphore()
    for peer in (sibling, partner1, partner2):
        pl.semaphore_signal(barrier, inc=1, device_id={"tensor": peer}, device_id_type=MESH)

    @pl.loop(1, owners)
    def _(i):
        peer = (expert + i) % owners
        pl.semaphore_signal(barrier, inc=1, device_id={"expert": peer}, device_id_type=MESH)

    ctx_copies = []
    for half, c_own in ((0, 1 - core), (1, core)):
        for place, dest in enumerate((chip3, chip1, chip2, chip)):
            rows = pl.ds(pl.multiple_of((dest * 2 + c_own) * 32, 32), 32)
            ctx_copies.append(
                pltpu.make_async_copy(
                    ctx_hbm.at[rows, :],
                    ctx_s.at[pl.ds(half * 128 + place * 32, 32), :],
                    ctx_sem.at[half * 4 + place],
                )
            )
    for copy in ctx_copies:
        copy.start()

    def w_copy(k, q):
        cols = pl.ds(pl.multiple_of(q * quarter + k * STRIP, 128), STRIP)
        return pltpu.make_async_copy(
            w_hbm.at[:, cols], w_s.at[k, :, pl.ds(q * STRIP, STRIP)], w_sem.at[k, q]
        )

    @pl.loop(0, chunks)
    def _(k):
        for q in range(4):
            w_copy(k, q).start()

    res_copy = pltpu.make_async_copy(res_hbm, res_s, res_sem)
    res_copy.start()
    bits_copy = pltpu.make_async_copy(bits_hbm, bits_s, bits_sem)
    bits_copy.start()
    small_copies = [
        pltpu.make_async_copy(src, dst, small_sem.at[i])
        for i, (src, dst) in enumerate(
            ((routes_hbm, routes_s), (bias_hbm, bias_b))
        )
    ]
    for copy in small_copies:
        copy.start()

    def matmul(k):
        for q in range(4):
            w_copy(k, q).wait()
        part = jnp.dot(ctx_s[...], w_s[k], preferred_element_type=F32).astype(BF16)
        a_send[k] = part[:128]
        a_own[k] = part[128:]

    def remote(src, dst, ssem, rsem, peer):
        return pltpu.make_async_remote_copy(
            src_ref=src, dst_ref=dst, send_sem=ssem, recv_sem=rsem,
            device_id={"tensor": peer}, device_id_type=MESH,
        )

    def a_copy(k):
        return remote(a_send.at[k], a_recv.at[k], a_ssem.at[k], a_rsem.at[k], sibling)

    def b_copy(k):
        return remote(b_send.at[k], b_recv.at[k], b_ssem.at[k], b_rsem.at[k], partner1)

    def c_copy(k):
        return remote(c_send.at[k], c_recv.at[k], c_ssem.at[k], c_rsem.at[k], partner2)

    def stage_b(k):
        a_copy(k).wait_recv()
        b_send[k] = (a_own[k, :64].astype(F32) + a_recv[k, :64].astype(F32)).astype(BF16)
        b_copy(k).start()
        b_keep[k] = a_own[k, 64:].astype(F32) + a_recv[k, 64:].astype(F32)

    def stage_c(k):
        b_copy(k).wait_recv()
        c_send[k] = (b_keep[k, :32] + b_recv[k, :32].astype(F32)).astype(BF16)
        c_copy(k).start()
        c_keep[k] = b_keep[k, 32:] + b_recv[k, 32:].astype(F32)

    def stage_x(k):
        c_copy(k).wait_recv()
        pieces = []
        for q in range(4):
            parts = []
            for i in range(STRIP // 128):
                block = q * (quarter // 128) + k * (STRIP // 128) + i
                cols = pl.ds(pl.multiple_of(block * 128, 128), 128)
                lanes = pl.ds(q * STRIP + i * 128, 128)
                total = c_keep[k, :, lanes] + c_recv[k, :, lanes].astype(F32)
                attention = total.astype(BF16).astype(F32)
                hidden = (
                    res_s[:, cols].astype(F32)
                    + (attention + bias_s[pl.ds(block, 1), :]) * mask_s[:, cols]
                ).astype(BF16)
                hid_s[:, cols] = hidden
                value = hidden.astype(F32)
                squares_s[...] += value * value
                parts.append(hidden)
            pieces.append(jnp.concatenate(parts, axis=1))
        stacked = jnp.concatenate(pieces, axis=0)
        picked = jnp.dot(select_s[...], stacked, preferred_element_type=F32).astype(BF16)
        cols = pl.ds(pl.multiple_of(k * STRIP, 128), STRIP)
        x_send[:, :, cols] = picked.reshape(owners, 16, STRIP)

        @pl.loop(1, owners)
        def _(i):
            peer = (expert + i) % owners
            pltpu.make_async_remote_copy(
                src_ref=x_send.at[peer, :, cols], dst_ref=x_recv.at[expert, :, cols],
                send_sem=x_ssem, recv_sem=x_rsem,
                device_id={"expert": peer}, device_id_type=MESH,
            ).start()

    for copy in ctx_copies:
        copy.wait()
    matmul(0)
    pl.semaphore_wait(barrier, owners + 2)
    a_copy(0).start()
    matmul(1)
    a_copy(1).start()
    stage_b(0)

    same_token = iota((32, 128), 1) % 32 == iota((32, 128), 0)
    for copy in small_copies:
        copy.wait()
    named_by = jnp.dot(
        routes_s[...].astype(F32).astype(BF16),
        jnp.where(same_token, 1.0, 0.0).astype(BF16),
        preferred_element_type=F32,
    )
    first, second = named_by[0:1], named_by[1:2]
    j0, j1 = iota((128, 128), 0), iota((128, 128), 1)
    before = jnp.where((j0 // 32 == j1 // 32) & (j0 % 32 < j1 % 32), 1.0, 0.0).astype(BF16)

    def chosen(named, slot):
        named = named.astype(F32)
        hits = jnp.where((first == named) | (second == named), 1.0, 0.0)
        earlier = jnp.dot(hits.astype(BF16), before, preferred_element_type=F32)
        return jnp.where(earlier == slot.astype(F32), hits, 0.0)

    row, lane = iota((owners * 16, 128), 0), iota((owners * 16, 128), 1)
    picks = chosen(2 * (row // 16) + (row % 4) // 2, row % 2)
    select_s[...] = jnp.where((row // 4) % 4 == lane // 32, picks, 0.0).astype(BF16)
    row, lane = iota((owners, 128), 0), iota((owners, 128), 1)
    for slot in range(4):
        picks = chosen(2 * row + slot // 2, jnp.full((owners, 128), slot % 2, jnp.int32))
        slots_s[slot] = jnp.where(lane < 32, picks, 0.0)

    bias_s[...] = bias_b[...].astype(F32)
    bits_copy.wait()
    squares_s[...] = jnp.zeros_like(squares_s)
    words = features // 16
    for start in range(0, words, 128):
        count = min(128, words - start)
        block = bits_s[:, start:start + count]
        low = (block % 256).astype(F32).astype(BF16)
        high = (block // 256).astype(F32).astype(BF16)
        spread_row, spread_col = iota((count, count * 16), 0), iota((count, count * 16), 1)
        here = spread_col // 16 == spread_row
        is_low = spread_col % 16 < 8
        spread_low = jnp.where(here & is_low, 1.0, 0.0).astype(BF16)
        spread_high = jnp.where(here & jnp.logical_not(is_low), 1.0, 0.0).astype(BF16)
        byte = jnp.dot(low, spread_low, preferred_element_type=F32) + jnp.dot(
            high, spread_high, preferred_element_type=F32
        )
        shift = iota(byte.shape, 1) % 8
        bit = jnp.bitwise_and(jnp.right_shift(byte.astype(jnp.int32), shift), 1)
        mask_s[:, start * 16:(start + count) * 16] = bit.astype(F32) * KEEP_SCALE
    res_copy.wait()

    @pl.loop(0, chunks + 1)
    def _(t):
        @pl.when(t >= 1)
        def _():
            stage_x(t - 1)

        @pl.when(t < chunks)
        def _():
            stage_c(t)

        @pl.when(t + 1 < chunks)
        def _():
            stage_b(t + 1)

        @pl.when(t + 2 < chunks)
        def _():
            matmul(t + 2)
            a_copy(t + 2).start()

    mean = jnp.sum(squares_s[...], axis=1, keepdims=True) / features
    scale = lax.rsqrt(mean + EPS)
    scale_row = jnp.sum(jnp.where(same_token, scale, 0.0), axis=0, keepdims=True)
    packed = jnp.zeros((owners, 128), F32)
    for slot in range(4):
        value = jnp.sum(slots_s[slot] * scale_row, axis=1, keepdims=True)
        packed = packed + jnp.where(lane == slot, value, 0.0)
    scl_s[...] = packed.reshape(owners, 1, 128)

    @pl.loop(1, owners)
    def _(i):
        peer = (expert + i) % owners
        pltpu.make_async_remote_copy(
            src_ref=scl_s.at[peer], dst_ref=scl_r.at[expert],
            send_sem=s_ssem, recv_sem=s_rsem,
            device_id={"expert": peer}, device_id_type=MESH,
        ).start()

    own_copy = pltpu.make_async_copy(x_send.at[expert], x_recv.at[expert], own_sem)
    own_copy.start()
    own_scl = pltpu.make_async_copy(scl_s.at[expert], scl_r.at[expert], own_scl_sem)
    own_scl.start()

    @pl.loop(0, chunks)
    def _(k):
        a_copy(k).wait_send()
        b_copy(k).wait_send()
        c_copy(k).wait_send()

    others = pl.ds(0, owners - 1)
    pltpu.make_async_copy(x_send.at[others], x_send.at[others], x_ssem).wait()
    pltpu.make_async_copy(scl_s.at[others], scl_s.at[others], s_ssem).wait()
    pltpu.make_async_copy(x_recv.at[others], x_recv.at[others], x_rsem).wait()
    pltpu.make_async_copy(scl_r.at[others], scl_r.at[others], s_rsem).wait()
    own_copy.wait()
    own_scl.wait()


def finish(
    owners, features,
    hid_hbm, x_hbm, scl_hbm, gain_hbm,
    hid_out, out_hbm,
    x_recv, scl_r, gain_b, gain_s, out_s,
    hid_sem, x_sem, small_sem, out_sem,
):
    quarter = features // 4
    groups = owners // 8
    hid_copy = pltpu.make_async_copy(hid_hbm, hid_out, hid_sem)
    scl_copy = pltpu.make_async_copy(scl_hbm, scl_r, small_sem.at[0])
    gain_copy = pltpu.make_async_copy(gain_hbm, gain_b, small_sem.at[1])
    x_copies = [
        pltpu.make_async_copy(x_hbm.at[pl.ds(g * 8, 8)], x_recv.at[pl.ds(g * 8, 8)], x_sem.at[g])
        for g in range(groups)
    ]
    out_copies = [
        pltpu.make_async_copy(out_s.at[pl.ds(g * 16, 16)], out_hbm.at[pl.ds(g * 16, 16)], out_sem.at[g])
        for g in range(groups)
    ]
    scl_copy.start()
    gain_copy.start()
    for copy in x_copies:
        copy.start()
    hid_copy.start()
    gain_copy.wait()
    gain_s[...] = gain_b[...].astype(F32)
    scl_copy.wait()

    rows_out = owners * 4
    spread = jnp.where(iota((rows_out, owners), 0) // 4 == iota((rows_out, owners), 1), 1.0, 0.0)
    spread = spread.astype(BF16)
    left = scl_r[...].reshape(owners, 128)
    per_row = jnp.zeros((rows_out, 128), F32)
    for _ in range(3):
        part = left.astype(BF16)
        left = left - part.astype(F32)
        per_row = per_row + jnp.dot(spread, part, preferred_element_type=F32)
    own_lane = iota((rows_out, 128), 1) == iota((rows_out, 128), 0) % 4
    column = jnp.sum(jnp.where(own_lane, per_row, 0.0), axis=1, keepdims=True)
    to, came = iota((128, 128), 0), iota((128, 128), 1)
    source_of = (to % 32) // 4 * 16 + to // 32 * 4 + to % 4
    reorder = jnp.where(source_of == came, 1.0, 0.0).astype(BF16)
    for group in range(owners // 8):
        x_copies[group].wait()
        scale = jnp.broadcast_to(column[group * 32:group * 32 + 32], (32, 128))

        @pl.loop(0, quarter // FINAL)
        def _(n):
            cols = pl.ds(pl.multiple_of(n * FINAL, 128), FINAL)
            rows = x_recv[group * 8:group * 8 + 8, :, cols].reshape(128, FINAL)
            moved = jnp.dot(reorder, rows, preferred_element_type=F32)
            for q in range(4):
                for i in range(FINAL // 128):
                    block = q * (quarter // 128) + n * (FINAL // 128) + i
                    value = moved[q * 32:q * 32 + 32, i * 128:i * 128 + 128]
                    value = value * scale * gain_s[pl.ds(block, 1), :]
                    cols_out = pl.ds(pl.multiple_of(block * 128, 128), 128)
                    out_s[group * 16:group * 16 + 16, :, cols_out] = (
                        value.astype(BF16).reshape(16, 2, 128)
                    )

        out_copies[group].start()
    hid_copy.wait()
    for copy in out_copies:
        copy.wait()


def local(owners, groups, context, out_weight, attn_bias, residual, dropout_bits, norm_gain, routes):
    depth, features = out_weight.shape
    rows = context.shape[0]
    tokens = residual.shape[0]
    quarter = features // 4
    chunks = quarter // STRIP
    wide = 4 * STRIP
    vmem, dma = pltpu.VMEM, pltpu.SemaphoreType.DMA
    hidden, sent, scales = pl.pallas_call(
        functools.partial(kernel, owners, groups, features),
        out_shape=(
            jax.ShapeDtypeStruct((tokens, features), BF16),
            jax.ShapeDtypeStruct((owners, 16, quarter), BF16),
            jax.ShapeDtypeStruct((owners, 1, 128), F32),
        ),
        in_specs=[pl.BlockSpec(memory_space=pltpu.HBM)] * 6,
        out_specs=[
            pl.BlockSpec(memory_space=pltpu.VMEM),
            pl.BlockSpec(memory_space=pltpu.HBM),
            pl.BlockSpec(memory_space=pltpu.HBM),
        ],
        scratch_shapes=[
            vmem((rows, depth), BF16),
            vmem((chunks, depth, wide), BF16),
            vmem((chunks, 128, wide), BF16),
            vmem((chunks, 128, wide), BF16),
            vmem((chunks, 128, wide), BF16),
            vmem((chunks, 64, wide), BF16),
            vmem((chunks, 64, wide), BF16),
            vmem((chunks, 64, wide), F32),
            vmem((chunks, 32, wide), BF16),
            vmem((chunks, 32, wide), BF16),
            vmem((chunks, 32, wide), F32),
            vmem((tokens, features), BF16),
            vmem((tokens, features // 16), jnp.int32),
            vmem((tokens, features), F32),
            vmem((owners * 16, 128), BF16),
            vmem((4, owners, 128), F32),
            vmem((tokens, 128), F32),
            vmem((owners, 16, quarter), BF16),
            vmem((owners, 1, 128), F32),
            vmem((features // 128, 128), BF16),
            vmem((2, tokens), jnp.int32),
            vmem((features // 128, 128), F32),
            dma((8,)),
            dma((chunks, 4)),
            dma, dma,
            dma((2,)),
            dma, dma,
            dma((chunks,)), dma((chunks,)),
            dma((chunks,)), dma((chunks,)),
            dma((chunks,)), dma((chunks,)),
            dma, dma, dma, dma,
        ],
        compiler_params=pltpu.CompilerParams(
            collective_id=0, has_side_effects=True, vmem_limit_bytes=60 * 1024 * 1024
        ),
        cost_estimate=pl.CostEstimate(
            flops=2 * rows * depth * features,
            bytes_accessed=2 * depth * features,
            transcendentals=0,
        ),
    )(context, out_weight, attn_bias.reshape(-1, 128), residual, dropout_bits, routes.T)
    hidden, normed = pl.pallas_call(
        functools.partial(finish, owners, features),
        out_shape=(
            jax.ShapeDtypeStruct((tokens, features), BF16),
            jax.ShapeDtypeStruct((owners * 2, 2, features), BF16),
        ),
        in_specs=[pl.BlockSpec(memory_space=pltpu.HBM)] * 4,
        out_specs=[pl.BlockSpec(memory_space=pltpu.HBM)] * 2,
        scratch_shapes=[
            vmem((owners, 16, quarter), BF16),
            vmem((owners, 1, 128), F32),
            vmem((features // 128, 128), BF16),
            vmem((features // 128, 128), F32),
            vmem((owners * 2, 2, features), BF16),
            dma,
            dma((owners // 8,)),
            dma((2,)),
            dma((owners // 8,)),
        ],
        compiler_params=pltpu.CompilerParams(vmem_limit_bytes=60 * 1024 * 1024),
    )(hidden, sent, scales, norm_gain.reshape(-1, 128))
    return hidden, normed.reshape(owners, 1, 2, 2, features)


def solution(mesh):
    owners, groups = mesh.shape["expert"], mesh.shape["tensor"]
    tokens_split = P(("dp", "expert", "tensor"), None)
    return jax.shard_map(
        functools.partial(local, owners, groups),
        mesh=mesh,
        in_specs=(
            P(("dp", "expert"), "tensor"), P("tensor", None), P(),
            tokens_split, tokens_split, P(), tokens_split,
        ),
        out_specs=(tokens_split, P("dp", "tensor", "expert", None, None)),
        check_vma=False,
    )
```

```python
import functools

import jax
import jax.numpy as jnp
from jax import lax
from jax.experimental import pallas as pl
from jax.experimental.pallas import tpu as pltpu
from jax.sharding import PartitionSpec as P

MESH = pl.DeviceIdType.MESH
KEEP_SCALE = 1.0 / 0.9
EPS = 1e-05
BF16 = jnp.bfloat16
F32 = jnp.float32

STRIP = 256
FINAL = 256


def iota(shape, dim):
    return lax.broadcasted_iota(jnp.int32, shape, dim)


def kernel(
    owners, groups, features,
    ctx_hbm, w_hbm, bias_hbm, res_hbm, bits_hbm, routes_hbm,
    hid_s, x_recv, scl_r,
    ctx_s, w_s, a_send, a_own, a_recv, b_send, b_recv, b_keep, c_send, c_recv, c_keep,
    res_s, bits_s, mask_s, select_s, slots_s, squares_s, x_send, scl_s,
    bias_b, routes_s, bias_s,
    ctx_sem, w_sem, res_sem, bits_sem, small_sem, own_sem, own_scl_sem,
    a_ssem, a_rsem, b_ssem, b_rsem, c_ssem, c_rsem, x_ssem, x_rsem, s_ssem, s_rsem,
):
    quarter = features // 4
    chunks = quarter // STRIP
    expert = lax.axis_index("expert")
    tensor = lax.axis_index("tensor")
    chip = tensor // 2
    core = tensor % 2
    sibling = chip * 2 + (1 - core)
    chip1 = chip + 1 - 2 * (chip % 2)
    chip2 = (chip + 2) % 4
    chip3 = 3 - chip
    partner1 = chip1 * 2 + core
    partner2 = chip2 * 2 + core

    barrier = pltpu.get_barrier_semaphore()
    for peer in (sibling, partner1, partner2):
        pl.semaphore_signal(barrier, inc=1, device_id={"tensor": peer}, device_id_type=MESH)

    @pl.loop(1, owners)
    def _(i):
        peer = (expert + i) % owners
        pl.semaphore_signal(barrier, inc=1, device_id={"expert": peer}, device_id_type=MESH)

    ctx_copies = []
    for half, c_own in ((0, 1 - core), (1, core)):
        for place, dest in enumerate((chip3, chip1, chip2, chip)):
            rows = pl.ds(pl.multiple_of((dest * 2 + c_own) * 32, 32), 32)
            ctx_copies.append(
                pltpu.make_async_copy(
                    ctx_hbm.at[rows, :],
                    ctx_s.at[pl.ds(half * 128 + place * 32, 32), :],
                    ctx_sem.at[half * 4 + place],
                )
            )
    for copy in ctx_copies:
        copy.start()

    def w_copy(k, q):
        cols = pl.ds(pl.multiple_of(q * quarter + k * STRIP, 128), STRIP)
        return pltpu.make_async_copy(
            w_hbm.at[:, cols], w_s.at[k, :, pl.ds(q * STRIP, STRIP)], w_sem.at[k, q]
        )

    @pl.loop(0, chunks)
    def _(k):
        for q in range(4):
            w_copy(k, q).start()

    res_copy = pltpu.make_async_copy(res_hbm, res_s, res_sem)
    res_copy.start()
    bits_copy = pltpu.make_async_copy(bits_hbm, bits_s, bits_sem)
    bits_copy.start()
    small_copies = [
        pltpu.make_async_copy(src, dst, small_sem.at[i])
        for i, (src, dst) in enumerate(
            ((routes_hbm, routes_s), (bias_hbm, bias_b))
        )
    ]
    for copy in small_copies:
        copy.start()

    def matmul(k):
        for q in range(4):
            w_copy(k, q).wait()
        part = jnp.dot(ctx_s[...], w_s[k], preferred_element_type=F32).astype(BF16)
        a_send[k] = part[:128]
        a_own[k] = part[128:]

    def remote(src, dst, ssem, rsem, peer):
        return pltpu.make_async_remote_copy(
            src_ref=src, dst_ref=dst, send_sem=ssem, recv_sem=rsem,
            device_id={"tensor": peer}, device_id_type=MESH,
        )

    def a_copy(k):
        return remote(a_send.at[k], a_recv.at[k], a_ssem.at[k], a_rsem.at[k], sibling)

    def b_copy(k):
        return remote(b_send.at[k], b_recv.at[k], b_ssem.at[k], b_rsem.at[k], partner1)

    def c_copy(k):
        return remote(c_send.at[k], c_recv.at[k], c_ssem.at[k], c_rsem.at[k], partner2)

    def stage_b(k):
        a_copy(k).wait_recv()
        b_send[k] = (a_own[k, :64].astype(F32) + a_recv[k, :64].astype(F32)).astype(BF16)
        b_copy(k).start()
        b_keep[k] = a_own[k, 64:].astype(F32) + a_recv[k, 64:].astype(F32)

    def stage_c(k):
        b_copy(k).wait_recv()
        c_send[k] = (b_keep[k, :32] + b_recv[k, :32].astype(F32)).astype(BF16)
        c_copy(k).start()
        c_keep[k] = b_keep[k, 32:] + b_recv[k, 32:].astype(F32)

    def stage_x(k):
        c_copy(k).wait_recv()
        pieces = []
        for q in range(4):
            parts = []
            for i in range(STRIP // 128):
                block = q * (quarter // 128) + k * (STRIP // 128) + i
                cols = pl.ds(pl.multiple_of(block * 128, 128), 128)
                lanes = pl.ds(q * STRIP + i * 128, 128)
                total = c_keep[k, :, lanes] + c_recv[k, :, lanes].astype(F32)
                attention = total.astype(BF16).astype(F32)
                hidden = (
                    res_s[:, cols].astype(F32)
                    + (attention + bias_s[pl.ds(block, 1), :]) * mask_s[:, cols]
                ).astype(BF16)
                hid_s[:, cols] = hidden
                value = hidden.astype(F32)
                squares_s[...] += value * value
                parts.append(hidden)
            pieces.append(jnp.concatenate(parts, axis=1))
        stacked = jnp.concatenate(pieces, axis=0)
        picked = jnp.dot(select_s[...], stacked, preferred_element_type=F32).astype(BF16)
        cols = pl.ds(pl.multiple_of(k * STRIP, 128), STRIP)
        x_send[:, :, cols] = picked.reshape(owners, 16, STRIP)

        @pl.loop(1, owners)
        def _(i):
            peer = (expert + i) % owners
            pltpu.make_async_remote_copy(
                src_ref=x_send.at[peer, :, cols], dst_ref=x_recv.at[expert, :, cols],
                send_sem=x_ssem, recv_sem=x_rsem,
                device_id={"expert": peer}, device_id_type=MESH,
            ).start()

    for copy in ctx_copies:
        copy.wait()
    matmul(0)
    pl.semaphore_wait(barrier, owners + 2)
    a_copy(0).start()
    matmul(1)
    a_copy(1).start()
    stage_b(0)

    same_token = iota((32, 128), 1) % 32 == iota((32, 128), 0)
    for copy in small_copies:
        copy.wait()
    named_by = jnp.dot(
        routes_s[...].astype(F32).astype(BF16),
        jnp.where(same_token, 1.0, 0.0).astype(BF16),
        preferred_element_type=F32,
    )
    first, second = named_by[0:1], named_by[1:2]
    j0, j1 = iota((128, 128), 0), iota((128, 128), 1)
    before = jnp.where((j0 // 32 == j1 // 32) & (j0 % 32 < j1 % 32), 1.0, 0.0).astype(BF16)

    def chosen(named, slot):
        named = named.astype(F32)
        hits = jnp.where((first == named) | (second == named), 1.0, 0.0)
        earlier = jnp.dot(hits.astype(BF16), before, preferred_element_type=F32)
        return jnp.where(earlier == slot.astype(F32), hits, 0.0)

    row, lane = iota((owners * 16, 128), 0), iota((owners * 16, 128), 1)
    picks = chosen(2 * (row // 16) + (row % 4) // 2, row % 2)
    select_s[...] = jnp.where((row // 4) % 4 == lane // 32, picks, 0.0).astype(BF16)
    row, lane = iota((owners, 128), 0), iota((owners, 128), 1)
    for slot in range(4):
        picks = chosen(2 * row + slot // 2, jnp.full((owners, 128), slot % 2, jnp.int32))
        slots_s[slot] = jnp.where(lane < 32, picks, 0.0)

    bias_s[...] = bias_b[...].astype(F32)
    bits_copy.wait()
    squares_s[...] = jnp.zeros_like(squares_s)
    words = features // 16
    for start in range(0, words, 128):
        count = min(128, words - start)
        block = bits_s[:, start:start + count]
        low = (block % 256).astype(F32).astype(BF16)
        high = (block // 256).astype(F32).astype(BF16)
        spread_row, spread_col = iota((count, count * 16), 0), iota((count, count * 16), 1)
        here = spread_col // 16 == spread_row
        is_low = spread_col % 16 < 8
        spread_low = jnp.where(here & is_low, 1.0, 0.0).astype(BF16)
        spread_high = jnp.where(here & jnp.logical_not(is_low), 1.0, 0.0).astype(BF16)
        byte = jnp.dot(low, spread_low, preferred_element_type=F32) + jnp.dot(
            high, spread_high, preferred_element_type=F32
        )
        shift = iota(byte.shape, 1) % 8
        bit = jnp.bitwise_and(jnp.right_shift(byte.astype(jnp.int32), shift), 1)
        mask_s[:, start * 16:(start + count) * 16] = bit.astype(F32) * KEEP_SCALE
    res_copy.wait()

    @pl.loop(0, chunks + 1)
    def _(t):
        @pl.when(t >= 1)
        def _():
            stage_x(t - 1)

        @pl.when(t < chunks)
        def _():
            stage_c(t)

        @pl.when(t + 1 < chunks)
        def _():
            stage_b(t + 1)

        @pl.when(t + 2 < chunks)
        def _():
            matmul(t + 2)
            a_copy(t + 2).start()

    mean = jnp.sum(squares_s[...], axis=1, keepdims=True) / features
    scale = lax.rsqrt(mean + EPS)
    scale_row = jnp.sum(jnp.where(same_token, scale, 0.0), axis=0, keepdims=True)
    packed = jnp.zeros((owners, 128), F32)
    for slot in range(4):
        value = jnp.sum(slots_s[slot] * scale_row, axis=1, keepdims=True)
        packed = packed + jnp.where(lane == slot, value, 0.0)
    scl_s[...] = packed.reshape(owners, 1, 128)

    @pl.loop(1, owners)
    def _(i):
        peer = (expert + i) % owners
        pltpu.make_async_remote_copy(
            src_ref=scl_s.at[peer], dst_ref=scl_r.at[expert],
            send_sem=s_ssem, recv_sem=s_rsem,
            device_id={"expert": peer}, device_id_type=MESH,
        ).start()

    own_copy = pltpu.make_async_copy(x_send.at[expert], x_recv.at[expert], own_sem)
    own_copy.start()
    own_scl = pltpu.make_async_copy(scl_s.at[expert], scl_r.at[expert], own_scl_sem)
    own_scl.start()

    @pl.loop(0, chunks)
    def _(k):
        a_copy(k).wait_send()
        b_copy(k).wait_send()
        c_copy(k).wait_send()

    others = pl.ds(0, owners - 1)
    pltpu.make_async_copy(x_send.at[others], x_send.at[others], x_ssem).wait()
    pltpu.make_async_copy(scl_s.at[others], scl_s.at[others], s_ssem).wait()
    pltpu.make_async_copy(x_recv.at[others], x_recv.at[others], x_rsem).wait()
    pltpu.make_async_copy(scl_r.at[others], scl_r.at[others], s_rsem).wait()
    own_copy.wait()
    own_scl.wait()


def finish(
    owners, features,
    hid_hbm, x_hbm, scl_hbm, gain_hbm,
    hid_out, out_hbm,
    x_recv, scl_r, gain_b, gain_s, out_s, hid_v,
    hid_sem, x_sem, small_sem, out_sem,
):
    quarter = features // 4
    groups = owners // 8
    hid_in = pltpu.make_async_copy(hid_hbm, hid_v, hid_sem.at[0])
    hid_copy = pltpu.make_async_copy(hid_v, hid_out, hid_sem.at[1])
    scl_copy = pltpu.make_async_copy(scl_hbm, scl_r, small_sem.at[0])
    gain_copy = pltpu.make_async_copy(gain_hbm, gain_b, small_sem.at[1])
    x_copies = [
        pltpu.make_async_copy(x_hbm.at[pl.ds(g * 8, 8)], x_recv.at[pl.ds(g * 8, 8)], x_sem.at[g])
        for g in range(groups)
    ]
    out_copies = [
        pltpu.make_async_copy(out_s.at[pl.ds(g * 16, 16)], out_hbm.at[pl.ds(g * 16, 16)], out_sem.at[g])
        for g in range(groups)
    ]
    scl_copy.start()
    gain_copy.start()
    for copy in x_copies:
        copy.start()
    hid_in.start()
    gain_copy.wait()
    gain_s[...] = gain_b[...].astype(F32)
    scl_copy.wait()
    hid_in.wait()
    hid_copy.start()

    rows_out = owners * 4
    spread = jnp.where(iota((rows_out, owners), 0) // 4 == iota((rows_out, owners), 1), 1.0, 0.0)
    spread = spread.astype(BF16)
    left = scl_r[...].reshape(owners, 128)
    per_row = jnp.zeros((rows_out, 128), F32)
    for _ in range(3):
        part = left.astype(BF16)
        left = left - part.astype(F32)
        per_row = per_row + jnp.dot(spread, part, preferred_element_type=F32)
    own_lane = iota((rows_out, 128), 1) == iota((rows_out, 128), 0) % 4
    column = jnp.sum(jnp.where(own_lane, per_row, 0.0), axis=1, keepdims=True)
    to, came = iota((128, 128), 0), iota((128, 128), 1)
    source_of = (to % 32) // 4 * 16 + to // 32 * 4 + to % 4
    reorder = jnp.where(source_of == came, 1.0, 0.0).astype(BF16)
    for group in range(owners // 8):
        x_copies[group].wait()
        scale = jnp.broadcast_to(column[group * 32:group * 32 + 32], (32, 128))

        @pl.loop(0, quarter // FINAL, unroll=True)
        def _(n):
            cols = pl.ds(pl.multiple_of(n * FINAL, 128), FINAL)
            rows = x_recv[group * 8:group * 8 + 8, :, cols].reshape(128, FINAL)
            moved = jnp.dot(reorder, rows, preferred_element_type=F32)
            for q in range(4):
                for i in range(FINAL // 128):
                    block = q * (quarter // 128) + n * (FINAL // 128) + i
                    value = moved[q * 32:q * 32 + 32, i * 128:i * 128 + 128]
                    value = value * scale * gain_s[pl.ds(block, 1), :]
                    cols_out = pl.ds(pl.multiple_of(block * 128, 128), 128)
                    out_s[group * 16:group * 16 + 16, :, cols_out] = (
                        value.astype(BF16).reshape(16, 2, 128)
                    )

        out_copies[group].start()
    hid_copy.wait()
    for copy in out_copies:
        copy.wait()


def local(owners, groups, context, out_weight, attn_bias, residual, dropout_bits, norm_gain, routes):
    depth, features = out_weight.shape
    rows = context.shape[0]
    tokens = residual.shape[0]
    quarter = features // 4
    chunks = quarter // STRIP
    wide = 4 * STRIP
    vmem, dma = pltpu.VMEM, pltpu.SemaphoreType.DMA
    hidden, sent, scales = pl.pallas_call(
        functools.partial(kernel, owners, groups, features),
        out_shape=(
            jax.ShapeDtypeStruct((tokens, features), BF16),
            jax.ShapeDtypeStruct((owners, 16, quarter), BF16),
            jax.ShapeDtypeStruct((owners, 1, 128), F32),
        ),
        in_specs=[pl.BlockSpec(memory_space=pltpu.HBM)] * 6,
        out_specs=[
            pl.BlockSpec(memory_space=pltpu.VMEM),
            pl.BlockSpec(memory_space=pltpu.HBM),
            pl.BlockSpec(memory_space=pltpu.HBM),
        ],
        scratch_shapes=[
            vmem((rows, depth), BF16),
            vmem((chunks, depth, wide), BF16),
            vmem((chunks, 128, wide), BF16),
            vmem((chunks, 128, wide), BF16),
            vmem((chunks, 128, wide), BF16),
            vmem((chunks, 64, wide), BF16),
            vmem((chunks, 64, wide), BF16),
            vmem((chunks, 64, wide), F32),
            vmem((chunks, 32, wide), BF16),
            vmem((chunks, 32, wide), BF16),
            vmem((chunks, 32, wide), F32),
            vmem((tokens, features), BF16),
            vmem((tokens, features // 16), jnp.int32),
            vmem((tokens, features), F32),
            vmem((owners * 16, 128), BF16),
            vmem((4, owners, 128), F32),
            vmem((tokens, 128), F32),
            vmem((owners, 16, quarter), BF16),
            vmem((owners, 1, 128), F32),
            vmem((features // 128, 128), BF16),
            vmem((2, tokens), jnp.int32),
            vmem((features // 128, 128), F32),
            dma((8,)),
            dma((chunks, 4)),
            dma, dma,
            dma((2,)),
            dma, dma,
            dma((chunks,)), dma((chunks,)),
            dma((chunks,)), dma((chunks,)),
            dma((chunks,)), dma((chunks,)),
            dma, dma, dma, dma,
        ],
        compiler_params=pltpu.CompilerParams(
            collective_id=0, has_side_effects=True, vmem_limit_bytes=60 * 1024 * 1024
        ),
        cost_estimate=pl.CostEstimate(
            flops=2 * rows * depth * features,
            bytes_accessed=2 * depth * features,
            transcendentals=0,
        ),
    )(context, out_weight, attn_bias.reshape(-1, 128), residual, dropout_bits, routes.T)
    hidden, normed = pl.pallas_call(
        functools.partial(finish, owners, features),
        out_shape=(
            jax.ShapeDtypeStruct((tokens, features), BF16),
            jax.ShapeDtypeStruct((owners * 2, 2, features), BF16),
        ),
        in_specs=[pl.BlockSpec(memory_space=pltpu.HBM)] * 4,
        out_specs=[pl.BlockSpec(memory_space=pltpu.HBM)] * 2,
        scratch_shapes=[
            vmem((owners, 16, quarter), BF16),
            vmem((owners, 1, 128), F32),
            vmem((features // 128, 128), BF16),
            vmem((features // 128, 128), F32),
            vmem((owners * 2, 2, features), BF16),
            vmem((tokens, features), BF16),
            dma((2,)),
            dma((owners // 8,)),
            dma((2,)),
            dma((owners // 8,)),
        ],
        compiler_params=pltpu.CompilerParams(vmem_limit_bytes=60 * 1024 * 1024),
    )(hidden, sent, scales, norm_gain.reshape(-1, 128))
    return hidden, normed.reshape(owners, 1, 2, 2, features)


def solution(mesh):
    owners, groups = mesh.shape["expert"], mesh.shape["tensor"]
    tokens_split = P(("dp", "expert", "tensor"), None)
    return jax.shard_map(
        functools.partial(local, owners, groups),
        mesh=mesh,
        in_specs=(
            P(("dp", "expert"), "tensor"), P("tensor", None), P(),
            tokens_split, tokens_split, P(), tokens_split,
        ),
        out_specs=(tokens_split, P("dp", "tensor", "expert", None, None)),
        check_vma=False,
    )
```

```python
import functools

import jax
import jax.numpy as jnp
from jax import lax
from jax.experimental import pallas as pl
from jax.experimental.pallas import tpu as pltpu
from jax.sharding import PartitionSpec as P

MESH = pl.DeviceIdType.MESH
KEEP_SCALE = 1.0 / 0.9
EPS = 1e-05
BF16 = jnp.bfloat16
F32 = jnp.float32

STRIP = 256
FINAL = 256


def iota(shape, dim):
    return lax.broadcasted_iota(jnp.int32, shape, dim)


def kernel(
    owners, groups, features,
    ctx_hbm, w_hbm, bias_hbm, res_hbm, bits_hbm, routes_hbm,
    hid_s, x_recv, scl_r,
    ctx_s, w_s, a_send, a_own, a_recv, b_send, b_recv, b_keep, c_send, c_recv, c_keep,
    res_s, bits_s, mask_s, select_s, slots_s, squares_s, x_send, scl_s,
    bias_b, routes_s, bias_s,
    ctx_sem, w_sem, res_sem, bits_sem, small_sem, own_sem, own_scl_sem,
    a_ssem, a_rsem, b_ssem, b_rsem, c_ssem, c_rsem, x_ssem, x_rsem, s_ssem, s_rsem,
):
    quarter = features // 4
    chunks = quarter // STRIP
    expert = lax.axis_index("expert")
    tensor = lax.axis_index("tensor")
    chip = tensor // 2
    core = tensor % 2
    sibling = chip * 2 + (1 - core)
    chip1 = chip + 1 - 2 * (chip % 2)
    chip2 = (chip + 2) % 4
    chip3 = 3 - chip
    partner1 = chip1 * 2 + core
    partner2 = chip2 * 2 + core

    barrier = pltpu.get_barrier_semaphore()
    for peer in (sibling, partner1, partner2):
        pl.semaphore_signal(barrier, inc=1, device_id={"tensor": peer}, device_id_type=MESH)

    @pl.loop(1, owners)
    def _(i):
        peer = (expert + i) % owners
        pl.semaphore_signal(barrier, inc=1, device_id={"expert": peer}, device_id_type=MESH)

    ctx_copies = []
    for half, c_own in ((0, 1 - core), (1, core)):
        for place, dest in enumerate((chip3, chip1, chip2, chip)):
            rows = pl.ds(pl.multiple_of((dest * 2 + c_own) * 32, 32), 32)
            ctx_copies.append(
                pltpu.make_async_copy(
                    ctx_hbm.at[rows, :],
                    ctx_s.at[pl.ds(half * 128 + place * 32, 32), :],
                    ctx_sem.at[half * 4 + place],
                )
            )
    for copy in ctx_copies:
        copy.start()

    def w_copy(k, q):
        cols = pl.ds(pl.multiple_of(q * quarter + k * STRIP, 128), STRIP)
        return pltpu.make_async_copy(
            w_hbm.at[:, cols], w_s.at[k, :, pl.ds(q * STRIP, STRIP)], w_sem.at[k, q]
        )

    @pl.loop(0, chunks)
    def _(k):
        for q in range(4):
            w_copy(k, q).start()

    res_copy = pltpu.make_async_copy(res_hbm, res_s, res_sem)
    res_copy.start()
    bits_copy = pltpu.make_async_copy(bits_hbm, bits_s, bits_sem)
    bits_copy.start()
    small_copies = [
        pltpu.make_async_copy(src, dst, small_sem.at[i])
        for i, (src, dst) in enumerate(
            ((routes_hbm, routes_s), (bias_hbm, bias_b))
        )
    ]
    for copy in small_copies:
        copy.start()

    def matmul(k):
        for q in range(4):
            w_copy(k, q).wait()
        part = jnp.dot(ctx_s[...], w_s[k], preferred_element_type=F32).astype(BF16)
        a_send[k] = part[:128]
        a_own[k] = part[128:]

    def remote(src, dst, ssem, rsem, peer):
        return pltpu.make_async_remote_copy(
            src_ref=src, dst_ref=dst, send_sem=ssem, recv_sem=rsem,
            device_id={"tensor": peer}, device_id_type=MESH,
        )

    def a_copy(k):
        return remote(a_send.at[k], a_recv.at[k], a_ssem.at[k], a_rsem.at[k], sibling)

    def b_copy(k):
        return remote(b_send.at[k], b_recv.at[k], b_ssem.at[k], b_rsem.at[k], partner1)

    def c_copy(k):
        return remote(c_send.at[k], c_recv.at[k], c_ssem.at[k], c_rsem.at[k], partner2)

    def stage_b(k):
        a_copy(k).wait_recv()
        b_send[k] = (a_own[k, :64].astype(F32) + a_recv[k, :64].astype(F32)).astype(BF16)
        b_copy(k).start()
        b_keep[k] = a_own[k, 64:].astype(F32) + a_recv[k, 64:].astype(F32)

    def stage_c(k):
        b_copy(k).wait_recv()
        c_send[k] = (b_keep[k, :32] + b_recv[k, :32].astype(F32)).astype(BF16)
        c_copy(k).start()
        c_keep[k] = b_keep[k, 32:] + b_recv[k, 32:].astype(F32)

    def stage_x(k):
        c_copy(k).wait_recv()
        pieces = []
        for q in range(4):
            parts = []
            for i in range(STRIP // 128):
                block = q * (quarter // 128) + k * (STRIP // 128) + i
                cols = pl.ds(pl.multiple_of(block * 128, 128), 128)
                lanes = pl.ds(q * STRIP + i * 128, 128)
                total = c_keep[k, :, lanes] + c_recv[k, :, lanes].astype(F32)
                attention = total.astype(BF16).astype(F32)
                hidden = (
                    res_s[:, cols].astype(F32)
                    + (attention + bias_s[pl.ds(block, 1), :]) * mask_s[:, cols]
                ).astype(BF16)
                hid_s[:, cols] = hidden
                value = hidden.astype(F32)
                squares_s[...] += value * value
                parts.append(hidden)
            pieces.append(jnp.concatenate(parts, axis=1))
        stacked = jnp.concatenate(pieces, axis=0)
        picked = jnp.dot(select_s[...], stacked, preferred_element_type=F32).astype(BF16)
        cols = pl.ds(pl.multiple_of(k * STRIP, 128), STRIP)
        x_send[:, :, cols] = picked.reshape(owners, 16, STRIP)

    def dispatch(first, width):
        cols = pl.ds(pl.multiple_of(first, 128), width)

        @pl.loop(1, owners)
        def _(i):
            peer = (expert + i) % owners
            pltpu.make_async_remote_copy(
                src_ref=x_send.at[peer, :, cols], dst_ref=x_recv.at[expert, :, cols],
                send_sem=x_ssem, recv_sem=x_rsem,
                device_id={"expert": peer}, device_id_type=MESH,
            ).start()

    for copy in ctx_copies:
        copy.wait()
    matmul(0)
    pl.semaphore_wait(barrier, owners + 2)
    a_copy(0).start()
    matmul(1)
    a_copy(1).start()
    stage_b(0)

    same_token = iota((32, 128), 1) % 32 == iota((32, 128), 0)
    for copy in small_copies:
        copy.wait()
    named_by = jnp.dot(
        routes_s[...].astype(F32).astype(BF16),
        jnp.where(same_token, 1.0, 0.0).astype(BF16),
        preferred_element_type=F32,
    )
    first, second = named_by[0:1], named_by[1:2]
    j0, j1 = iota((128, 128), 0), iota((128, 128), 1)
    before = jnp.where((j0 // 32 == j1 // 32) & (j0 % 32 < j1 % 32), 1.0, 0.0).astype(BF16)

    def chosen(named, slot):
        named = named.astype(F32)
        hits = jnp.where((first == named) | (second == named), 1.0, 0.0)
        earlier = jnp.dot(hits.astype(BF16), before, preferred_element_type=F32)
        return jnp.where(earlier == slot.astype(F32), hits, 0.0)

    row, lane = iota((owners * 16, 128), 0), iota((owners * 16, 128), 1)
    picks = chosen(2 * (row // 16) + (row % 4) // 2, row % 2)
    select_s[...] = jnp.where((row // 4) % 4 == lane // 32, picks, 0.0).astype(BF16)
    row, lane = iota((owners, 128), 0), iota((owners, 128), 1)
    for slot in range(4):
        picks = chosen(2 * row + slot // 2, jnp.full((owners, 128), slot % 2, jnp.int32))
        slots_s[slot] = jnp.where(lane < 32, picks, 0.0)

    bias_s[...] = bias_b[...].astype(F32)
    bits_copy.wait()
    squares_s[...] = jnp.zeros_like(squares_s)
    words = features // 16
    for start in range(0, words, 128):
        count = min(128, words - start)
        block = bits_s[:, start:start + count]
        low = (block % 256).astype(F32).astype(BF16)
        high = (block // 256).astype(F32).astype(BF16)
        spread_row, spread_col = iota((count, count * 16), 0), iota((count, count * 16), 1)
        here = spread_col // 16 == spread_row
        is_low = spread_col % 16 < 8
        spread_low = jnp.where(here & is_low, 1.0, 0.0).astype(BF16)
        spread_high = jnp.where(here & jnp.logical_not(is_low), 1.0, 0.0).astype(BF16)
        byte = jnp.dot(low, spread_low, preferred_element_type=F32) + jnp.dot(
            high, spread_high, preferred_element_type=F32
        )
        shift = iota(byte.shape, 1) % 8
        bit = jnp.bitwise_and(jnp.right_shift(byte.astype(jnp.int32), shift), 1)
        mask_s[:, start * 16:(start + count) * 16] = bit.astype(F32) * KEEP_SCALE
    res_copy.wait()

    @pl.loop(0, chunks + 1)
    def _(t):
        @pl.when(t >= 1)
        def _():
            stage_x(t - 1)

        @pl.when(t == 1)
        def _():
            dispatch(0, STRIP)

        @pl.when((t > 1) & (t % 2 == 1))
        def _():
            dispatch((t - 2) * STRIP, 2 * STRIP)

        @pl.when(t < chunks)
        def _():
            stage_c(t)

        @pl.when(t + 1 < chunks)
        def _():
            stage_b(t + 1)

        @pl.when(t + 2 < chunks)
        def _():
            matmul(t + 2)
            a_copy(t + 2).start()

    mean = jnp.sum(squares_s[...], axis=1, keepdims=True) / features
    scale = lax.rsqrt(mean + EPS)
    scale_row = jnp.sum(jnp.where(same_token, scale, 0.0), axis=0, keepdims=True)
    packed = jnp.zeros((owners, 128), F32)
    for slot in range(4):
        value = jnp.sum(slots_s[slot] * scale_row, axis=1, keepdims=True)
        packed = packed + jnp.where(lane == slot, value, 0.0)
    scl_s[...] = packed.reshape(owners, 1, 128)

    @pl.loop(1, owners)
    def _(i):
        peer = (expert + i) % owners
        pltpu.make_async_remote_copy(
            src_ref=scl_s.at[peer], dst_ref=scl_r.at[expert],
            send_sem=s_ssem, recv_sem=s_rsem,
            device_id={"expert": peer}, device_id_type=MESH,
        ).start()

    own_copy = pltpu.make_async_copy(x_send.at[expert], x_recv.at[expert], own_sem)
    own_copy.start()
    own_scl = pltpu.make_async_copy(scl_s.at[expert], scl_r.at[expert], own_scl_sem)
    own_scl.start()

    @pl.loop(0, chunks)
    def _(k):
        a_copy(k).wait_send()
        b_copy(k).wait_send()
        c_copy(k).wait_send()

    others = pl.ds(0, owners - 1)
    pltpu.make_async_copy(x_send.at[others], x_send.at[others], x_ssem).wait()
    pltpu.make_async_copy(scl_s.at[others], scl_s.at[others], s_ssem).wait()
    pltpu.make_async_copy(x_recv.at[others], x_recv.at[others], x_rsem).wait()
    pltpu.make_async_copy(scl_r.at[others], scl_r.at[others], s_rsem).wait()
    own_copy.wait()
    own_scl.wait()


def finish(
    owners, features,
    hid_hbm, x_hbm, scl_hbm, gain_hbm,
    hid_out, out_hbm,
    x_recv, scl_r, gain_b, gain_s, out_s, hid_v,
    hid_sem, x_sem, small_sem, out_sem,
):
    quarter = features // 4
    groups = owners // 8
    hid_in = pltpu.make_async_copy(hid_hbm, hid_v, hid_sem.at[0])
    hid_copy = pltpu.make_async_copy(hid_v, hid_out, hid_sem.at[1])
    scl_copy = pltpu.make_async_copy(scl_hbm, scl_r, small_sem.at[0])
    gain_copy = pltpu.make_async_copy(gain_hbm, gain_b, small_sem.at[1])
    x_copies = [
        pltpu.make_async_copy(x_hbm.at[pl.ds(g * 8, 8)], x_recv.at[pl.ds(g * 8, 8)], x_sem.at[g])
        for g in range(groups)
    ]
    out_copies = [
        pltpu.make_async_copy(out_s.at[pl.ds(g * 16, 16)], out_hbm.at[pl.ds(g * 16, 16)], out_sem.at[g])
        for g in range(groups)
    ]
    scl_copy.start()
    gain_copy.start()
    for copy in x_copies:
        copy.start()
    hid_in.start()
    gain_copy.wait()
    gain_s[...] = gain_b[...].astype(F32)
    scl_copy.wait()
    hid_in.wait()
    hid_copy.start()

    rows_out = owners * 4
    spread = jnp.where(iota((rows_out, owners), 0) // 4 == iota((rows_out, owners), 1), 1.0, 0.0)
    spread = spread.astype(BF16)
    left = scl_r[...].reshape(owners, 128)
    per_row = jnp.zeros((rows_out, 128), F32)
    for _ in range(3):
        part = left.astype(BF16)
        left = left - part.astype(F32)
        per_row = per_row + jnp.dot(spread, part, preferred_element_type=F32)
    own_lane = iota((rows_out, 128), 1) == iota((rows_out, 128), 0) % 4
    column = jnp.sum(jnp.where(own_lane, per_row, 0.0), axis=1, keepdims=True)
    to, came = iota((128, 128), 0), iota((128, 128), 1)
    source_of = (to % 32) // 4 * 16 + to // 32 * 4 + to % 4
    reorder = jnp.where(source_of == came, 1.0, 0.0).astype(BF16)
    for group in range(owners // 8):
        x_copies[group].wait()
        scale = jnp.broadcast_to(column[group * 32:group * 32 + 32], (32, 128))

        @pl.loop(0, quarter // FINAL, unroll=True)
        def _(n):
            cols = pl.ds(pl.multiple_of(n * FINAL, 128), FINAL)
            rows = x_recv[group * 8:group * 8 + 8, :, cols].reshape(128, FINAL)
            moved = jnp.dot(reorder, rows, preferred_element_type=F32)
            for q in range(4):
                for i in range(FINAL // 128):
                    block = q * (quarter // 128) + n * (FINAL // 128) + i
                    value = moved[q * 32:q * 32 + 32, i * 128:i * 128 + 128]
                    value = value * scale * gain_s[pl.ds(block, 1), :]
                    cols_out = pl.ds(pl.multiple_of(block * 128, 128), 128)
                    out_s[group * 16:group * 16 + 16, :, cols_out] = (
                        value.astype(BF16).reshape(16, 2, 128)
                    )

        out_copies[group].start()
    hid_copy.wait()
    for copy in out_copies:
        copy.wait()


def local(owners, groups, context, out_weight, attn_bias, residual, dropout_bits, norm_gain, routes):
    depth, features = out_weight.shape
    rows = context.shape[0]
    tokens = residual.shape[0]
    quarter = features // 4
    chunks = quarter // STRIP
    wide = 4 * STRIP
    vmem, dma = pltpu.VMEM, pltpu.SemaphoreType.DMA
    hidden, sent, scales = pl.pallas_call(
        functools.partial(kernel, owners, groups, features),
        out_shape=(
            jax.ShapeDtypeStruct((tokens, features), BF16),
            jax.ShapeDtypeStruct((owners, 16, quarter), BF16),
            jax.ShapeDtypeStruct((owners, 1, 128), F32),
        ),
        in_specs=[pl.BlockSpec(memory_space=pltpu.HBM)] * 6,
        out_specs=[
            pl.BlockSpec(memory_space=pltpu.VMEM),
            pl.BlockSpec(memory_space=pltpu.HBM),
            pl.BlockSpec(memory_space=pltpu.HBM),
        ],
        scratch_shapes=[
            vmem((rows, depth), BF16),
            vmem((chunks, depth, wide), BF16),
            vmem((chunks, 128, wide), BF16),
            vmem((chunks, 128, wide), BF16),
            vmem((chunks, 128, wide), BF16),
            vmem((chunks, 64, wide), BF16),
            vmem((chunks, 64, wide), BF16),
            vmem((chunks, 64, wide), F32),
            vmem((chunks, 32, wide), BF16),
            vmem((chunks, 32, wide), BF16),
            vmem((chunks, 32, wide), F32),
            vmem((tokens, features), BF16),
            vmem((tokens, features // 16), jnp.int32),
            vmem((tokens, features), F32),
            vmem((owners * 16, 128), BF16),
            vmem((4, owners, 128), F32),
            vmem((tokens, 128), F32),
            vmem((owners, 16, quarter), BF16),
            vmem((owners, 1, 128), F32),
            vmem((features // 128, 128), BF16),
            vmem((2, tokens), jnp.int32),
            vmem((features // 128, 128), F32),
            dma((8,)),
            dma((chunks, 4)),
            dma, dma,
            dma((2,)),
            dma, dma,
            dma((chunks,)), dma((chunks,)),
            dma((chunks,)), dma((chunks,)),
            dma((chunks,)), dma((chunks,)),
            dma, dma, dma, dma,
        ],
        compiler_params=pltpu.CompilerParams(
            collective_id=0, has_side_effects=True, vmem_limit_bytes=60 * 1024 * 1024
        ),
        cost_estimate=pl.CostEstimate(
            flops=2 * rows * depth * features,
            bytes_accessed=2 * depth * features,
            transcendentals=0,
        ),
    )(context, out_weight, attn_bias.reshape(-1, 128), residual, dropout_bits, routes.T)
    hidden, normed = pl.pallas_call(
        functools.partial(finish, owners, features),
        out_shape=(
            jax.ShapeDtypeStruct((tokens, features), BF16),
            jax.ShapeDtypeStruct((owners * 2, 2, features), BF16),
        ),
        in_specs=[pl.BlockSpec(memory_space=pltpu.HBM)] * 4,
        out_specs=[pl.BlockSpec(memory_space=pltpu.HBM)] * 2,
        scratch_shapes=[
            vmem((owners, 16, quarter), BF16),
            vmem((owners, 1, 128), F32),
            vmem((features // 128, 128), BF16),
            vmem((features // 128, 128), F32),
            vmem((owners * 2, 2, features), BF16),
            vmem((tokens, features), BF16),
            dma((2,)),
            dma((owners // 8,)),
            dma((2,)),
            dma((owners // 8,)),
        ],
        compiler_params=pltpu.CompilerParams(vmem_limit_bytes=60 * 1024 * 1024),
    )(hidden, sent, scales, norm_gain.reshape(-1, 128))
    return hidden, normed.reshape(owners, 1, 2, 2, features)


def solution(mesh):
    owners, groups = mesh.shape["expert"], mesh.shape["tensor"]
    tokens_split = P(("dp", "expert", "tensor"), None)
    return jax.shard_map(
        functools.partial(local, owners, groups),
        mesh=mesh,
        in_specs=(
            P(("dp", "expert"), "tensor"), P("tensor", None), P(),
            tokens_split, tokens_split, P(), tokens_split,
        ),
        out_specs=(tokens_split, P("dp", "tensor", "expert", None, None)),
        check_vma=False,
    )
```

```python
import functools

import jax
import jax.numpy as jnp
from jax import lax
from jax.experimental import pallas as pl
from jax.experimental.pallas import tpu as pltpu
from jax.sharding import PartitionSpec as P

MESH = pl.DeviceIdType.MESH
KEEP_SCALE = 1.0 / 0.9
EPS = 1e-05
BF16 = jnp.bfloat16
F32 = jnp.float32

STRIP = 256
FINAL = 256


def iota(shape, dim):
    return lax.broadcasted_iota(jnp.int32, shape, dim)


def kernel(
    owners, groups, features,
    ctx_hbm, w_hbm, bias_hbm, res_hbm, bits_hbm, routes_hbm,
    hid_s, x_recv, scl_r,
    ctx_s, w_s, a_send, a_own, a_recv, b_send, b_recv, b_keep, c_send, c_recv, c_keep,
    res_s, bits_s, mask_s, select_s, slots_s, squares_s, x_send, scl_s,
    bias_b, routes_s, bias_s,
    ctx_sem, w_sem, res_sem, bits_sem, small_sem, own_sem, own_scl_sem,
    a_ssem, a_rsem, b_ssem, b_rsem, c_ssem, c_rsem, x_ssem, x_rsem, s_ssem, s_rsem,
):
    quarter = features // 4
    chunks = quarter // STRIP
    expert = lax.axis_index("expert")
    tensor = lax.axis_index("tensor")
    chip = tensor // 2
    core = tensor % 2
    sibling = chip * 2 + (1 - core)
    chip1 = chip + 1 - 2 * (chip % 2)
    chip2 = (chip + 2) % 4
    chip3 = 3 - chip
    partner1 = chip1 * 2 + core
    partner2 = chip2 * 2 + core

    barrier = pltpu.get_barrier_semaphore()
    for peer in (sibling, partner1, partner2):
        pl.semaphore_signal(barrier, inc=1, device_id={"tensor": peer}, device_id_type=MESH)

    @pl.loop(1, owners)
    def _(i):
        peer = (expert + i) % owners
        pl.semaphore_signal(barrier, inc=1, device_id={"expert": peer}, device_id_type=MESH)

    ctx_copies = []
    for half, c_own in ((0, 1 - core), (1, core)):
        for place, dest in enumerate((chip3, chip1, chip2, chip)):
            rows = pl.ds(pl.multiple_of((dest * 2 + c_own) * 32, 32), 32)
            ctx_copies.append(
                pltpu.make_async_copy(
                    ctx_hbm.at[rows, :],
                    ctx_s.at[pl.ds(half * 128 + place * 32, 32), :],
                    ctx_sem.at[half * 4 + place],
                )
            )
    for copy in ctx_copies:
        copy.start()

    def w_copy(k, q):
        cols = pl.ds(pl.multiple_of(q * quarter + k * STRIP, 128), STRIP)
        return pltpu.make_async_copy(
            w_hbm.at[:, cols], w_s.at[k, :, pl.ds(q * STRIP, STRIP)], w_sem.at[k, q]
        )

    @pl.loop(0, chunks)
    def _(k):
        for q in range(4):
            w_copy(k, q).start()

    res_copy = pltpu.make_async_copy(res_hbm, res_s, res_sem)
    res_copy.start()
    bits_copy = pltpu.make_async_copy(bits_hbm, bits_s, bits_sem)
    bits_copy.start()
    small_copies = [
        pltpu.make_async_copy(src, dst, small_sem.at[i])
        for i, (src, dst) in enumerate(
            ((routes_hbm, routes_s), (bias_hbm, bias_b))
        )
    ]
    for copy in small_copies:
        copy.start()

    def matmul(k):
        for q in range(4):
            w_copy(k, q).wait()
        part = jnp.dot(ctx_s[...], w_s[k], preferred_element_type=F32).astype(BF16)
        a_send[k] = part[:128]
        a_own[k] = part[128:]

    def remote(src, dst, ssem, rsem, peer):
        return pltpu.make_async_remote_copy(
            src_ref=src, dst_ref=dst, send_sem=ssem, recv_sem=rsem,
            device_id={"tensor": peer}, device_id_type=MESH,
        )

    def a_copy(k):
        return remote(a_send.at[k], a_recv.at[k], a_ssem.at[k], a_rsem.at[k], sibling)

    def b_copy(k):
        return remote(b_send.at[k], b_recv.at[k], b_ssem.at[k], b_rsem.at[k], partner1)

    def c_copy(k):
        return remote(c_send.at[k], c_recv.at[k], c_ssem.at[k], c_rsem.at[k], partner2)

    def stage_b(k):
        a_copy(k).wait_recv()
        b_send[k] = (a_own[k, :64].astype(F32) + a_recv[k, :64].astype(F32)).astype(BF16)
        b_copy(k).start()
        b_keep[k] = a_own[k, 64:].astype(F32) + a_recv[k, 64:].astype(F32)

    def stage_c(k):
        b_copy(k).wait_recv()
        c_send[k] = (b_keep[k, :32] + b_recv[k, :32].astype(F32)).astype(BF16)
        c_copy(k).start()
        c_keep[k] = b_keep[k, 32:] + b_recv[k, 32:].astype(F32)

    def stage_x(k):
        c_copy(k).wait_recv()
        pieces = []
        for q in range(4):
            parts = []
            for i in range(STRIP // 128):
                block = q * (quarter // 128) + k * (STRIP // 128) + i
                cols = pl.ds(pl.multiple_of(block * 128, 128), 128)
                lanes = pl.ds(q * STRIP + i * 128, 128)
                total = c_keep[k, :, lanes] + c_recv[k, :, lanes].astype(F32)
                attention = total.astype(BF16).astype(F32)
                hidden = (
                    res_s[:, cols].astype(F32)
                    + (attention + bias_s[pl.ds(block, 1), :]) * mask_s[:, cols]
                ).astype(BF16)
                hid_s[:, cols] = hidden
                value = hidden.astype(F32)
                squares_s[...] += value * value
                parts.append(hidden)
            pieces.append(jnp.concatenate(parts, axis=1))
        stacked = jnp.concatenate(pieces, axis=0)
        picked = jnp.dot(select_s[...], stacked, preferred_element_type=F32).astype(BF16)
        cols = pl.ds(pl.multiple_of(k * STRIP, 128), STRIP)
        x_send[:, :, cols] = picked.reshape(owners, 16, STRIP)

        @pl.loop(1, owners)
        def _(i):
            peer = (expert + i) % owners
            pltpu.make_async_remote_copy(
                src_ref=x_send.at[peer, :, cols], dst_ref=x_recv.at[expert, :, cols],
                send_sem=x_ssem, recv_sem=x_rsem,
                device_id={"expert": peer}, device_id_type=MESH,
            ).start()

    for copy in ctx_copies:
        copy.wait()
    matmul(0)
    pl.semaphore_wait(barrier, owners + 2)
    a_copy(0).start()
    matmul(1)
    a_copy(1).start()
    stage_b(0)

    same_token = iota((32, 128), 1) % 32 == iota((32, 128), 0)
    for copy in small_copies:
        copy.wait()
    named_by = jnp.dot(
        routes_s[...].astype(F32).astype(BF16),
        jnp.where(same_token, 1.0, 0.0).astype(BF16),
        preferred_element_type=F32,
    )
    first, second = named_by[0:1], named_by[1:2]
    j0, j1 = iota((128, 128), 0), iota((128, 128), 1)
    before = jnp.where((j0 // 32 == j1 // 32) & (j0 % 32 < j1 % 32), 1.0, 0.0).astype(BF16)

    def chosen(named, slot):
        named = named.astype(F32)
        hits = jnp.where((first == named) | (second == named), 1.0, 0.0)
        earlier = jnp.dot(hits.astype(BF16), before, preferred_element_type=F32)
        return jnp.where(earlier == slot.astype(F32), hits, 0.0)

    row, lane = iota((owners * 16, 128), 0), iota((owners * 16, 128), 1)
    picks = chosen(2 * (row // 16) + (row % 4) // 2, row % 2)
    select_s[...] = jnp.where((row // 4) % 4 == lane // 32, picks, 0.0).astype(BF16)
    row, lane = iota((owners, 128), 0), iota((owners, 128), 1)
    for slot in range(4):
        picks = chosen(2 * row + slot // 2, jnp.full((owners, 128), slot % 2, jnp.int32))
        slots_s[slot] = jnp.where(lane < 32, picks, 0.0)

    bias_s[...] = bias_b[...].astype(F32)
    bits_copy.wait()
    squares_s[...] = jnp.zeros_like(squares_s)
    words = features // 16
    for start in range(0, words, 128):
        count = min(128, words - start)
        block = bits_s[:, start:start + count]
        low = (block % 256).astype(F32).astype(BF16)
        high = (block // 256).astype(F32).astype(BF16)
        spread_row, spread_col = iota((count, count * 16), 0), iota((count, count * 16), 1)
        here = spread_col // 16 == spread_row
        is_low = spread_col % 16 < 8
        spread_low = jnp.where(here & is_low, 1.0, 0.0).astype(BF16)
        spread_high = jnp.where(here & jnp.logical_not(is_low), 1.0, 0.0).astype(BF16)
        byte = jnp.dot(low, spread_low, preferred_element_type=F32) + jnp.dot(
            high, spread_high, preferred_element_type=F32
        )
        shift = iota(byte.shape, 1) % 8
        bit = jnp.bitwise_and(jnp.right_shift(byte.astype(jnp.int32), shift), 1)
        mask_s[:, start * 16:(start + count) * 16] = bit.astype(F32) * KEEP_SCALE
    res_copy.wait()

    @pl.loop(0, chunks + 2)
    def _(t):
        @pl.when(t >= 2)
        def _():
            stage_x(t - 2)

        @pl.when((t >= 1) & (t <= chunks))
        def _():
            stage_c(t - 1)

        @pl.when(t + 1 < chunks)
        def _():
            stage_b(t + 1)

        @pl.when(t + 2 < chunks)
        def _():
            matmul(t + 2)
            a_copy(t + 2).start()

    mean = jnp.sum(squares_s[...], axis=1, keepdims=True) / features
    scale = lax.rsqrt(mean + EPS)
    scale_row = jnp.sum(jnp.where(same_token, scale, 0.0), axis=0, keepdims=True)
    packed = jnp.zeros((owners, 128), F32)
    for slot in range(4):
        value = jnp.sum(slots_s[slot] * scale_row, axis=1, keepdims=True)
        packed = packed + jnp.where(lane == slot, value, 0.0)
    scl_s[...] = packed.reshape(owners, 1, 128)

    @pl.loop(1, owners)
    def _(i):
        peer = (expert + i) % owners
        pltpu.make_async_remote_copy(
            src_ref=scl_s.at[peer], dst_ref=scl_r.at[expert],
            send_sem=s_ssem, recv_sem=s_rsem,
            device_id={"expert": peer}, device_id_type=MESH,
        ).start()

    own_copy = pltpu.make_async_copy(x_send.at[expert], x_recv.at[expert], own_sem)
    own_copy.start()
    own_scl = pltpu.make_async_copy(scl_s.at[expert], scl_r.at[expert], own_scl_sem)
    own_scl.start()

    @pl.loop(0, chunks)
    def _(k):
        a_copy(k).wait_send()
        b_copy(k).wait_send()
        c_copy(k).wait_send()

    others = pl.ds(0, owners - 1)
    pltpu.make_async_copy(x_send.at[others], x_send.at[others], x_ssem).wait()
    pltpu.make_async_copy(scl_s.at[others], scl_s.at[others], s_ssem).wait()
    pltpu.make_async_copy(x_recv.at[others], x_recv.at[others], x_rsem).wait()
    pltpu.make_async_copy(scl_r.at[others], scl_r.at[others], s_rsem).wait()
    own_copy.wait()
    own_scl.wait()


def finish(
    owners, features,
    hid_hbm, x_hbm, scl_hbm, gain_hbm,
    hid_out, out_hbm,
    x_recv, scl_r, gain_b, gain_s, out_s, hid_v,
    hid_sem, x_sem, small_sem, out_sem,
):
    quarter = features // 4
    groups = owners // 8
    hid_in = pltpu.make_async_copy(hid_hbm, hid_v, hid_sem.at[0])
    hid_copy = pltpu.make_async_copy(hid_v, hid_out, hid_sem.at[1])
    scl_copy = pltpu.make_async_copy(scl_hbm, scl_r, small_sem.at[0])
    gain_copy = pltpu.make_async_copy(gain_hbm, gain_b, small_sem.at[1])
    x_copies = [
        pltpu.make_async_copy(x_hbm.at[pl.ds(g * 8, 8)], x_recv.at[pl.ds(g * 8, 8)], x_sem.at[g])
        for g in range(groups)
    ]
    out_copies = [
        pltpu.make_async_copy(out_s.at[pl.ds(g * 16, 16)], out_hbm.at[pl.ds(g * 16, 16)], out_sem.at[g])
        for g in range(groups)
    ]
    scl_copy.start()
    gain_copy.start()
    for copy in x_copies:
        copy.start()
    hid_in.start()
    gain_copy.wait()
    gain_s[...] = gain_b[...].astype(F32)
    scl_copy.wait()
    hid_in.wait()
    hid_copy.start()

    rows_out = owners * 4
    spread = jnp.where(iota((rows_out, owners), 0) // 4 == iota((rows_out, owners), 1), 1.0, 0.0)
    spread = spread.astype(BF16)
    left = scl_r[...].reshape(owners, 128)
    per_row = jnp.zeros((rows_out, 128), F32)
    for _ in range(3):
        part = left.astype(BF16)
        left = left - part.astype(F32)
        per_row = per_row + jnp.dot(spread, part, preferred_element_type=F32)
    own_lane = iota((rows_out, 128), 1) == iota((rows_out, 128), 0) % 4
    column = jnp.sum(jnp.where(own_lane, per_row, 0.0), axis=1, keepdims=True)
    to, came = iota((128, 128), 0), iota((128, 128), 1)
    source_of = (to % 32) // 4 * 16 + to // 32 * 4 + to % 4
    reorder = jnp.where(source_of == came, 1.0, 0.0).astype(BF16)
    for group in range(owners // 8):
        x_copies[group].wait()
        scale = jnp.broadcast_to(column[group * 32:group * 32 + 32], (32, 128))

        @pl.loop(0, quarter // FINAL, unroll=True)
        def _(n):
            cols = pl.ds(pl.multiple_of(n * FINAL, 128), FINAL)
            rows = x_recv[group * 8:group * 8 + 8, :, cols].reshape(128, FINAL)
            moved = jnp.dot(reorder, rows, preferred_element_type=F32)
            for q in range(4):
                for i in range(FINAL // 128):
                    block = q * (quarter // 128) + n * (FINAL // 128) + i
                    value = moved[q * 32:q * 32 + 32, i * 128:i * 128 + 128]
                    value = value * scale * gain_s[pl.ds(block, 1), :]
                    cols_out = pl.ds(pl.multiple_of(block * 128, 128), 128)
                    out_s[group * 16:group * 16 + 16, :, cols_out] = (
                        value.astype(BF16).reshape(16, 2, 128)
                    )

        out_copies[group].start()
    hid_copy.wait()
    for copy in out_copies:
        copy.wait()


def local(owners, groups, context, out_weight, attn_bias, residual, dropout_bits, norm_gain, routes):
    depth, features = out_weight.shape
    rows = context.shape[0]
    tokens = residual.shape[0]
    quarter = features // 4
    chunks = quarter // STRIP
    wide = 4 * STRIP
    vmem, dma = pltpu.VMEM, pltpu.SemaphoreType.DMA
    hidden, sent, scales = pl.pallas_call(
        functools.partial(kernel, owners, groups, features),
        out_shape=(
            jax.ShapeDtypeStruct((tokens, features), BF16),
            jax.ShapeDtypeStruct((owners, 16, quarter), BF16),
            jax.ShapeDtypeStruct((owners, 1, 128), F32),
        ),
        in_specs=[pl.BlockSpec(memory_space=pltpu.HBM)] * 6,
        out_specs=[
            pl.BlockSpec(memory_space=pltpu.VMEM),
            pl.BlockSpec(memory_space=pltpu.HBM),
            pl.BlockSpec(memory_space=pltpu.HBM),
        ],
        scratch_shapes=[
            vmem((rows, depth), BF16),
            vmem((chunks, depth, wide), BF16),
            vmem((chunks, 128, wide), BF16),
            vmem((chunks, 128, wide), BF16),
            vmem((chunks, 128, wide), BF16),
            vmem((chunks, 64, wide), BF16),
            vmem((chunks, 64, wide), BF16),
            vmem((chunks, 64, wide), F32),
            vmem((chunks, 32, wide), BF16),
            vmem((chunks, 32, wide), BF16),
            vmem((chunks, 32, wide), F32),
            vmem((tokens, features), BF16),
            vmem((tokens, features // 16), jnp.int32),
            vmem((tokens, features), F32),
            vmem((owners * 16, 128), BF16),
            vmem((4, owners, 128), F32),
            vmem((tokens, 128), F32),
            vmem((owners, 16, quarter), BF16),
            vmem((owners, 1, 128), F32),
            vmem((features // 128, 128), BF16),
            vmem((2, tokens), jnp.int32),
            vmem((features // 128, 128), F32),
            dma((8,)),
            dma((chunks, 4)),
            dma, dma,
            dma((2,)),
            dma, dma,
            dma((chunks,)), dma((chunks,)),
            dma((chunks,)), dma((chunks,)),
            dma((chunks,)), dma((chunks,)),
            dma, dma, dma, dma,
        ],
        compiler_params=pltpu.CompilerParams(
            collective_id=0, has_side_effects=True, vmem_limit_bytes=60 * 1024 * 1024
        ),
        cost_estimate=pl.CostEstimate(
            flops=2 * rows * depth * features,
            bytes_accessed=2 * depth * features,
            transcendentals=0,
        ),
    )(context, out_weight, attn_bias.reshape(-1, 128), residual, dropout_bits, routes.T)
    hidden, normed = pl.pallas_call(
        functools.partial(finish, owners, features),
        out_shape=(
            jax.ShapeDtypeStruct((tokens, features), BF16),
            jax.ShapeDtypeStruct((owners * 2, 2, features), BF16),
        ),
        in_specs=[pl.BlockSpec(memory_space=pltpu.HBM)] * 4,
        out_specs=[pl.BlockSpec(memory_space=pltpu.HBM)] * 2,
        scratch_shapes=[
            vmem((owners, 16, quarter), BF16),
            vmem((owners, 1, 128), F32),
            vmem((features // 128, 128), BF16),
            vmem((features // 128, 128), F32),
            vmem((owners * 2, 2, features), BF16),
            vmem((tokens, features), BF16),
            dma((2,)),
            dma((owners // 8,)),
            dma((2,)),
            dma((owners // 8,)),
        ],
        compiler_params=pltpu.CompilerParams(vmem_limit_bytes=60 * 1024 * 1024),
    )(hidden, sent, scales, norm_gain.reshape(-1, 128))
    return hidden, normed.reshape(owners, 1, 2, 2, features)


def solution(mesh):
    owners, groups = mesh.shape["expert"], mesh.shape["tensor"]
    tokens_split = P(("dp", "expert", "tensor"), None)
    return jax.shard_map(
        functools.partial(local, owners, groups),
        mesh=mesh,
        in_specs=(
            P(("dp", "expert"), "tensor"), P("tensor", None), P(),
            tokens_split, tokens_split, P(), tokens_split,
        ),
        out_specs=(tokens_split, P("dp", "tensor", "expert", None, None)),
        check_vma=False,
    )
```
